512 devices in a mesh: lat: 32 (over z_lo, y), lon: 16 (over z_hi, x, core).
Axes of the slice: x: 4, y: 4, z: 16 (z_hi: 2, z_lo: 8; z = z_hi * 8 + z_lo), core: 2. Of those that a mesh axis runs over, the one named last changes fastest.
Arguments:
- field: float32 [64, 1024, 2048], P(None, 'lat', 'lon'), may hold values from -6 to 6
- cotangent: float32 [64, 1024, 2048], P(None, 'lat', 'lon'), may hold values from -6 to 6
- w_approx: float32 [64, 64, 64, 128], P(None, None, 'lat', 'lon'), may hold values from -0.75 to 0.75
- w_detail: float32 [3, 64, 64, 64, 128], P(None, None, None, 'lat', 'lon'), may hold values from -0.75 to 0.75
- w_point: float32 [64, 64], replicated, may hold values from -0.75 to 0.75
- bias: float32 [64], replicated, may hold values from -4 to 4
Outputs:
- grad_field: float32 [64, 1024, 2048], P(None, 'lat', 'lon')
- grad_approx: float32 [64, 64, 64, 128], P(None, None, 'lat', 'lon')
- grad_detail: float32 [3, 64, 64, 64, 128], P(None, None, None, 'lat', 'lon')
- grad_point: float32 [64, 64], replicated
- grad_bias: float32 [64], replicated
The draws below stay inside these ranges and needn't reach their ends.
All inputs are finite; a program needn't handle non-finite values.
Results may differ from the reference program's by a relative error of at most 0.00016.
Values sent between devices are 32-bit elements; how exact they have to be, the bound alone decides.
A program may use at most 128 MiB of HBM per device.

```python
import jax
import jax.numpy as jnp
from jax import lax

C = 64
NLAT = 1024
NLON = 2048
MLAT = 64
MLON = 128


def shard_levels(stream_key, shape, cuts, least, largest):
    def one(axis_at, blocks):
        draws = jax.random.uniform(jax.random.fold_in(jax.random.fold_in(stream_key, 6), axis_at), (blocks,), jnp.float32, least / len(cuts), largest / len(cuts))
        return jnp.repeat(jnp.exp(draws), shape[axis_at] // blocks).reshape((-1,) + (1,) * (len(shape) - axis_at - 1))

    level = one(*cuts[0])
    for cut in cuts[1:]:
        level = level * one(*cut)
    return level


def normal_values(stream_key, shape, deviation, bound, shards=(), held_as=jnp.bfloat16):
    result = deviation * jax.random.normal(stream_key, shape, jnp.float32)
    if shards:
        result = result * shard_levels(stream_key, shape, shards, -0.22, 0.18)
    return jnp.clip(result, -bound, bound).astype(held_as)


def setup_inputs(seed: int = 0) -> dict:
    arg_keys = jax.random.split(jax.random.key(seed), 7)
    field = normal_values(arg_keys[0], (C, NLAT, NLON), 1.0, 6.0, ((1, 32), (2, 16)), jnp.float32)
    cotangent = normal_values(arg_keys[1], (C, NLAT, NLON), 1.0, 6.0, ((1, 32), (2, 16)), jnp.float32)
    w_approx = normal_values(arg_keys[2], (C, C, MLAT, MLON), C ** -0.5, 0.75, ((2, 32), (3, 16)), jnp.float32)
    w_detail = normal_values(arg_keys[3], (3, C, C, MLAT, MLON), C ** -0.5, 0.75, ((3, 32), (4, 16)), jnp.float32)
    w_point = normal_values(arg_keys[4], (C, C), C ** -0.5, 0.75, (), jnp.float32)
    bias = normal_values(arg_keys[5], (C,), 0.7, 4.0, (), jnp.float32)
    return dict(field=field, cotangent=cotangent, w_approx=w_approx, w_detail=w_detail, w_point=w_point, bias=bias)


low_taps = [0.23037781330885523, 0.7148465705525415, 0.6308807679295904, -0.02798376941698385, -0.18703481171888114, 0.030841381835986965, 0.032883011666982945, -0.010597401784997278]
high_taps = [low_taps[7 - j] if j % 2 == 0 else -low_taps[7 - j] for j in range(8)]

def split_axis(extended, axis, count):
    span = 2 * count + 6
    evens = lax.slice_in_dim(extended, 0, span, 2, axis)
    odds = lax.slice_in_dim(extended, 1, span, 2, axis)
    lowpart = None
    highpart = None
    for shift in range(4):
        even_part = lax.slice_in_dim(evens, shift, shift + count, 1, axis)
        odd_part = lax.slice_in_dim(odds, shift, shift + count, 1, axis)
        low_term = low_taps[2 * shift] * even_part + low_taps[2 * shift + 1] * odd_part
        high_term = high_taps[2 * shift] * even_part + high_taps[2 * shift + 1] * odd_part
        lowpart = low_term if lowpart is None else lowpart + low_term
        highpart = high_term if highpart is None else highpart + high_term
    return (lowpart, highpart)

def join_axis(low_ext, high_ext, axis, count):
    evens = None
    odds = None
    for shift in range(4):
        low_part = lax.slice_in_dim(low_ext, 3 - shift, 3 - shift + count, 1, axis)
        high_part = lax.slice_in_dim(high_ext, 3 - shift, 3 - shift + count, 1, axis)
        even_term = low_taps[2 * shift] * low_part + high_taps[2 * shift] * high_part
        odd_term = low_taps[2 * shift + 1] * low_part + high_taps[2 * shift + 1] * high_part
        evens = even_term if evens is None else evens + even_term
        odds = odd_term if odds is None else odds + odd_term
    joined = jnp.stack([evens, odds], axis + 1)
    shape = list(evens.shape)
    shape[axis] = 2 * count
    return joined.reshape(shape)

def analysis_level(block):
    height, width = (block.shape[1], block.shape[2])
    lat_ext = jnp.concatenate([block, block[:, :6]], 1)
    lowpart, highpart = split_axis(lat_ext, 1, height // 2)
    bands = []
    for part in (lowpart, highpart):
        lon_ext = jnp.concatenate([part, part[:, :, :6]], 2)
        bands.extend(split_axis(lon_ext, 2, width // 2))
    return bands

def synthesis_level(stacked):
    rows, cols = (stacked.shape[2], stacked.shape[3])
    lon_ext = jnp.concatenate([stacked[:, :, :, -3:], stacked], 3)
    lowpart = join_axis(lon_ext[0], lon_ext[1], 2, cols)
    highpart = join_axis(lon_ext[2], lon_ext[3], 2, cols)
    lowpart = jnp.concatenate([lowpart[:, -3:], lowpart], 1)
    highpart = jnp.concatenate([highpart[:, -3:], highpart], 1)
    return join_axis(lowpart, highpart, 1, rows)

def forward(field, w_approx, w_detail, w_point, bias):
    approx = field
    details = []
    for level in range(4):
        bands = analysis_level(approx)
        details.append(jnp.stack(bands[1:]))
        approx = bands[0]
    coarse = jnp.concatenate([approx[None], details[3]], 0)
    weights = jnp.concatenate([w_approx[None], w_detail], 0)
    mixed = jnp.einsum('bcij,bcoij->boij', coarse, weights, precision=lax.Precision.HIGHEST)
    branch = synthesis_level(mixed)
    for level in (2, 1, 0):
        branch = synthesis_level(jnp.concatenate([branch[None], details[level]], 0))
    pointwise = jnp.einsum('oc,chw->ohw', w_point, field, precision=lax.Precision.HIGHEST)
    pre = branch + pointwise + bias[:, None, None]
    return jax.nn.gelu(pre, approximate=False)

def reference(field, cotangent, w_approx, w_detail, w_point, bias):
    output, pullback = jax.vjp(forward, field, w_approx, w_detail, w_point, bias)
    grad_field, grad_approx, grad_detail, grad_point, grad_bias = pullback(cotangent)
    return (grad_field, grad_approx, grad_detail, grad_point, grad_bias)
```

```python
import math

import numpy as np

import jax
import jax.numpy as jnp
from jax import lax
from jax.experimental import pallas as pl
from jax.experimental.pallas import tpu as pltpu
from jax.sharding import PartitionSpec as P

LOW = np.array(
    [
        0.23037781330885523,
        0.7148465705525415,
        0.6308807679295904,
        -0.02798376941698385,
        -0.18703481171888114,
        0.030841381835986965,
        0.032883011666982945,
        -0.010597401784997278,
    ],
    np.float64,
)
HIGH = np.array([LOW[7 - j] if j % 2 == 0 else -LOW[7 - j] for j in range(8)])

C = 64
H = 32
W = 128
LAT = 32
LON = 16
PAIRS = H // 2
F32 = jnp.float32
BF16 = jnp.bfloat16
MESH = pl.DeviceIdType.MESH


def long_filters():
    def spread(taps, step):
        out = np.zeros((len(taps) - 1) * step + 1)
        out[::step] = taps
        return out

    third = np.ones(1)
    for level in range(3):
        third = np.convolve(third, spread(LOW, 2**level))
    return [np.convolve(third, spread(LOW, 8)), np.convolve(third, spread(HIGH, 8))]


def tap(taps, at):
    return taps[at] if 0 <= at < len(taps) else 0.0


def tables():
    both = long_filters()
    lat = np.zeros((PAIRS, 4, 2, 2, 2, C))
    for h2 in range(PAIRS):
        for dl in range(4):
            for u in range(2):
                for ii in range(2):
                    for p in range(2):
                        lat[h2, dl, u, ii, p, :] = tap(both[u], 2 * h2 + p + 32 * dl - 16 * ii)
    lat = lat.reshape(PAIRS * 16, 2 * C).astype(np.float32)
    lon = np.zeros((2, 2, 8, W))
    for ds in range(2):
        for v in range(2):
            for jj in range(8):
                for w in range(W):
                    lon[ds, v, jj, w] = tap(both[v], w + 128 * ds - 16 * jj)
    lon = lon.reshape(32, W).astype(np.float32)
    high = lon.astype(jnp.bfloat16).astype(np.float32)
    rest = (lon - high).astype(jnp.bfloat16).astype(np.float32)
    split = np.concatenate(
        [np.concatenate([high, high], 1), np.concatenate([rest, np.zeros_like(rest)], 1)], 0
    )
    join = np.concatenate([high, rest, high], 0)
    return lat, split, join


def halves(x):
    high = x.astype(BF16)
    return high, (x - high.astype(F32)).astype(BF16)


def swap(x):
    return pltpu.roll(x, 64, axis=1)


def dot_nt(a, b):
    return lax.dot_general(a, b, (((1,), (1,)), ((), ())), preferred_element_type=F32)


def dot_tn(a, b):
    return lax.dot_general(a, b, (((0,), (0,)), ((), ())), preferred_element_type=F32)


def gelu_slope(p):
    cdf = 0.5 * (1.0 + lax.erf(p * (1.0 / math.sqrt(2.0))))
    pdf = jnp.exp(-0.5 * p * p) * (1.0 / math.sqrt(2.0 * math.pi))
    return cdf + p * pdf


def kernel(
    field, cot, wa, wd, wpoint, bias, lat_hbm, split_hbm, join_hbm,
    out_field, out_ga, out_gd, out_gp, out_gb,
    fbuf, cbuf, wbuf, wpbuf, biasbuf, lat_tab, split_tab, join_tab,
    wfwd, wbwd, base, grad, thl, ghl, yscr, dup,
    send1, send2, send3, send4, recv1, recv2, recv3, recv4, coarse,
    gwbuf, obuf, gpbuf, gbbuf, red1, red2, red3, red4,
    load_sem, fload_sem, store_sem, ostore_sem, send_sem, recv_sem, rsend_sem, rrecv_sem,
):
    lat_at = lax.axis_index("lat")
    lon_at = lax.axis_index("lon")
    left = lax.broadcasted_iota(jnp.int32, (32, 2 * C), 1) < C

    steps = [(dl, ds) for dl in (3, 2, 1, 0) for ds in (1, 0) if (dl, ds) != (0, 0)]
    behind = [(lax.rem(lat_at + (LAT - dl), LAT), lax.rem(lon_at + (LON - ds), LON)) for dl, ds in steps]
    ahead = [(lax.rem(lat_at + dl, LAT), lax.rem(lon_at + ds, LON)) for dl, ds in steps]
    k_at = lax.rem(lon_at, 8)
    zhi = lon_at // 8
    y_at = lax.rem(lat_at, 4)
    zlo = lat_at // 4
    q_at = zhi * 4 + y_at
    k_peers = [lax.rem(k_at + d, 8) for d in range(1, 8)]
    q_peers = [lax.rem(q_at + d, 8) for d in range(1, 8)]
    z_peers = [lax.rem(zlo + d, 8) for d in range(1, 8)]
    k_ids = [(lat_at, zhi * 8 + k) for k in k_peers]
    q_ids = [(zlo * 4 + lax.rem(q, 4), (q // 4) * 8 + k_at) for q in q_peers]
    z_ids = [(z * 4 + y_at, lon_at) for z in z_peers]

    barrier = pltpu.get_barrier_semaphore()
    everyone = behind + ahead + k_ids + q_ids + z_ids

    field_loads = [
        pltpu.make_async_copy(field.at[:, pl.ds(8 * q, 8), :], fbuf.at[q], fload_sem.at[q]) for q in range(4)
    ]
    for load in field_loads:
        load.start()
    split_load = pltpu.make_async_copy(split_hbm, split_tab, load_sem.at[0])
    lat_load = pltpu.make_async_copy(lat_hbm, lat_tab, load_sem.at[1])
    wp_load = pltpu.make_async_copy(wpoint, wpbuf, load_sem.at[2])
    bias_load = pltpu.make_async_copy(bias, biasbuf, load_sem.at[3])
    wa_load = pltpu.make_async_copy(wa, wbuf.at[0], load_sem.at[4])
    wd_load = pltpu.make_async_copy(wd, wbuf.at[pl.ds(1, 3)], load_sem.at[5])
    cot_loads = [
        pltpu.make_async_copy(cot.at[:, pl.ds(8 * q, 8), :], cbuf.at[q], fload_sem.at[4 + q]) for q in range(4)
    ]
    join_load = pltpu.make_async_copy(join_hbm, join_tab, load_sem.at[6])
    for load in [split_load, lat_load, wp_load, bias_load, wa_load, wd_load, join_load] + cot_loads:
        load.start()
    for device in everyone:
        pl.semaphore_signal(barrier, inc=1, device_id=device, device_id_type=MESH)

    def cell_pair(buffer, h2):
        chunk, row = h2 // 4, (h2 % 4) * 2
        flat = buffer.at[chunk].reshape(C * 8, W)
        return jnp.concatenate([flat[pl.ds(row + p, C, stride=8), :] for p in range(2)], 0)

    def lon_split(rows, at):
        both = dot_nt(split_tab[...].astype(BF16), rows)
        sums = both[:32] + both[32:]
        yscr[at, :, :] = sums[:, :128]
        yscr[at + 1, :, :] = sums[:, 128:]

    def lat_split(buffer, on_block):
        for dl in (3, 2, 1, 0):
            def step(g, sums, dl=dl):
                sums = list(sums)
                for n in range(4):
                    h2 = g * 4 + n
                    y = yscr[h2]
                    for m in range(4):
                        sums[m] = sums[m] + lat_tab[pl.ds(h2 * 16 + dl * 4 + m, 1), :] * y
                return tuple(sums)

            zero = jnp.zeros((32, 2 * C), F32)
            sums = lax.fori_loop(0, 4, step, (zero,) * 4)
            for u in range(2):
                first, second = sums[2 * u], sums[2 * u + 1]
                modes = jnp.where(left, first, second) + swap(jnp.where(left, second, first))
                for ds in range(2):
                    buffer[dl * 2 + ds, u * 16:(u + 1) * 16, :] = modes[ds * 16:(ds + 1) * 16]
            on_block(dl)

    def exchange(number, source_of, recv, targets):
        return [
            pltpu.make_async_remote_copy(
                src_ref=source_of(dl * 2 + ds),
                dst_ref=recv.at[dl * 2 + ds],
                send_sem=send_sem.at[number, n],
                recv_sem=recv_sem.at[number, n],
                device_id=targets[n],
                device_id_type=MESH,
            )
            for n, (dl, ds) in enumerate(steps)
        ]

    def start_block(copies):
        def on_block(dl):
            for n, step in enumerate(steps):
                if step[0] == dl:
                    copies[n].start()
        return on_block

    def lat_join(recv, own):
        for dl in range(4):
            blocks = [own[...] if (dl, ds) == (0, 0) else recv[dl * 2 + ds] for ds in range(2)]
            for u in range(2):
                rows = jnp.concatenate([b[u * 16:(u + 1) * 16] for b in blocks], 0)
                turned = swap(rows)
                dup[dl * 4 + u * 2] = jnp.where(left, rows, turned)
                dup[dl * 4 + u * 2 + 1] = jnp.where(left, turned, rows)

    def lon_join(h2):
        total = jnp.zeros((32, 2 * C), F32)
        for m in range(16):
            total = total + lat_tab[pl.ds(h2 * 16 + m, 1), :] * dup[m]
        high, rest = halves(total)
        return dot_tn(jnp.concatenate([high, high, rest], 0), join_tab[...].astype(BF16))

    def point_map(weights, rows):
        high = [rows[64 * n:64 * n + 64, :W] for n in range(4)]
        rest = [rows[64 * n:64 * n + 64, W:] for n in range(4)]
        high = jnp.concatenate(high, 1)
        rest = jnp.concatenate(rest, 1)
        out = dot_tn(weights, jnp.concatenate([high, rest, high], 0))
        return jnp.concatenate([out[:, W * n:W * n + W] for n in range(4)], 0)

    split_load.wait()
    for q in range(4):
        field_loads[q].wait()
        for n in range(2):
            h2 = q * 4 + n * 2
            for k in range(2):
                high, rest = halves(cell_pair(fbuf, h2 + k))
                thl[(h2 + k) * 128:(h2 + k + 1) * 128, :W] = high
                thl[(h2 + k) * 128:(h2 + k + 1) * 128, W:] = rest
            lon_split(thl[h2 * 128:h2 * 128 + 256, :], h2)
    lat_load.wait()
    pl.semaphore_wait(barrier, len(everyone))
    copies1 = exchange(0, lambda n: send1.at[n], recv1, behind)
    lat_split(send1, start_block(copies1))

    wp_load.wait()
    bias_load.wait()
    high, rest = halves(wpbuf[...])
    wbwd[...] = jnp.concatenate([high, high, rest], 0)
    high, rest = halves(wpbuf[...].T)
    wfwd[...] = jnp.concatenate([high, high, rest], 0)
    bias_cells = jnp.broadcast_to(biasbuf[...], (W, C)).T
    bias_cells = jnp.concatenate([bias_cells, bias_cells], 0)
    for h4 in range(PAIRS // 2):
        mapped = point_map(wfwd[...], thl[h4 * 256:h4 * 256 + 256, :])
        for k in range(2):
            h2 = 2 * h4 + k
            base[h2] = mapped[128 * k:128 * k + 128] + cell_pair(fbuf, h2) + bias_cells
    wa_load.wait()
    wd_load.wait()

    total = send1[0]
    for n, (dl, ds) in enumerate(steps):
        copies1[n].wait_recv()
        total = total + recv1[dl * 2 + ds]
    coarse[...] = total

    def mix(g, carry):
        turned, sums = carry
        sums = list(sums)
        for k in range(8):
            for b in range(4):
                rows = turned[8 * b:8 * b + 8]
                column = jnp.concatenate([rows[:, k:k + 1], rows[:, C + k:C + k + 1]], 0)
                sums[b] = sums[b] + column * wbuf[b, g * 8 + k]
        return pltpu.roll(turned, 2 * C - 8, axis=1), tuple(sums)

    def packed(parts):
        return jnp.concatenate([jnp.concatenate([p[:8], p[8:]], 1) for p in parts], 0)

    _, mixed = lax.fori_loop(0, C // 8, mix, (total, (jnp.zeros((16, C), F32),) * 4))
    send2[...] = packed(mixed) - total
    copies2 = exchange(1, lambda n: send2, recv2, ahead)
    for copy in copies2:
        copy.start()

    join_load.wait()
    for load in cot_loads:
        load.wait()
    for copy in copies2:
        copy.wait_recv()
    lat_join(recv2, send2)

    for h4 in range(PAIRS // 2):
        for k in range(2):
            h2 = 2 * h4 + k
            g = gelu_slope(base[h2] + lon_join(h2)) * cell_pair(cbuf, h2)
            grad[h2] = g
            high, rest = halves(g)
            ghl[h2 * 128:(h2 + 1) * 128, :W] = high
            ghl[h2 * 128:(h2 + 1) * 128, W:] = rest
        lon_split(ghl[h4 * 256:h4 * 256 + 256, :], 2 * h4)
    copies3 = exchange(2, lambda n: send3.at[n], recv3, behind)
    lat_split(send3, start_block(copies3))

    point = jnp.zeros((128, 128), F32)
    rows_sum = jnp.zeros((C, W), F32)
    for h2 in range(PAIRS):
        at = h2 * 128
        both = []
        for source in (ghl, thl):
            tops = jnp.concatenate([source[at:at + 64, :W], source[at + 64:at + 128, :W]], 1)
            rests = jnp.concatenate([source[at:at + 64, W:], source[at + 64:at + 128, W:]], 1)
            both.append(jnp.concatenate([tops, rests], 0))
        point = point + dot_nt(both[0], both[1])
        rows_sum = rows_sum + grad[h2, 0:64, :] + grad[h2, 64:128, :]
    point = point[:C] + point[C:]
    point = point + swap(point)
    bias_term = jnp.sum(rows_sum, axis=1, keepdims=True)
    lane = lax.broadcasted_iota(jnp.int32, (C, 128), 1)
    gpbuf[...] = jnp.where(lane < C, point, jnp.where(lane == C, bias_term, 0.0))

    def reduce_copies(number, pairs, ids):
        return [
            pltpu.make_async_remote_copy(
                src_ref=src,
                dst_ref=dst,
                send_sem=rsend_sem.at[number, n],
                recv_sem=rrecv_sem.at[number, n],
                device_id=ids[n],
                device_id_type=MESH,
            )
            for n, (src, dst) in enumerate(pairs)
        ]

    def tile(ref, n):
        return ref.at[pl.ds(pl.multiple_of(8 * n, 8), 8)]

    def total8(ref):
        out = ref[0:8]
        for n in range(1, 8):
            out = out + ref[8 * n:8 * n + 8]
        return out

    red1[pl.ds(pl.multiple_of(8 * k_at, 8), 8), :] = gpbuf[pl.ds(pl.multiple_of(8 * k_at, 8), 8), :]
    reduce1 = reduce_copies(0, [(tile(gpbuf, k), tile(red1, k_at)) for k in k_peers], k_ids)
    for copy in reduce1:
        copy.start()

    for h4 in range(PAIRS // 2):
        mapped = point_map(wbwd[...], ghl[h4 * 256:h4 * 256 + 256, :])
        for k in range(2):
            h2 = 2 * h4 + k
            base[h2] = mapped[128 * k:128 * k + 128] + grad[h2]

    gtotal = send3[0]
    for n, (dl, ds) in enumerate(steps):
        copies3[n].wait_recv()
        gtotal = gtotal + recv3[dl * 2 + ds]

    def unpacked(rows, b):
        part = rows[8 * b:8 * b + 8]
        return jnp.concatenate([part[:, :C], part[:, C:]], 0)

    gmodes = [unpacked(gtotal, b) for b in range(4)]
    lanes16 = lax.broadcasted_iota(jnp.int32, (16, C), 1)

    def back(g, sums):
        sums = list(sums)
        for k in range(8):
            for b in range(4):
                one = jnp.sum(wbuf[b, g * 8 + k] * gmodes[b], axis=1, keepdims=True)
                sums[b] = jnp.where(lanes16 == g * 8 + k, one, sums[b])
        return tuple(sums)

    backs = lax.fori_loop(0, C // 8, back, (jnp.zeros((16, C), F32),) * 4)
    send4[...] = packed(backs) - gtotal
    copies4 = exchange(3, lambda n: send4, recv4, ahead)
    for copy in copies4:
        copy.start()

    for copy in reduce1:
        copy.wait_recv()
    red2[pl.ds(pl.multiple_of(8 * q_at, 8), 8), :] = total8(red1)
    reduce2 = reduce_copies(1, [(tile(red2, q_at), tile(red2, q_at))] * 7, q_ids)
    for copy in reduce2:
        copy.start()

    def outer(g, turned):
        for k in range(8):
            for b in range(4):
                rows = turned[8 * b:8 * b + 8]
                column = jnp.concatenate([rows[:, k:k + 1], rows[:, C + k:C + k + 1]], 0)
                gwbuf[b, g * 8 + k] = column * gmodes[b]
        return pltpu.roll(turned, 2 * C - 8, axis=1)

    lax.fori_loop(0, C // 8, outer, coarse[...])
    stores = [
        pltpu.make_async_copy(gwbuf.at[0], out_ga, store_sem.at[0]),
        pltpu.make_async_copy(gwbuf.at[pl.ds(1, 3)], out_gd, store_sem.at[1]),
    ]
    for store in stores:
        store.start()
    for copy in reduce2:
        copy.wait_recv()
    red3[pl.ds(pl.multiple_of(8 * zlo, 8), 8), :] = total8(red2)
    reduce3 = reduce_copies(2, [(tile(red3, zlo), tile(red3, zlo))] * 7, z_ids)
    for copy in reduce3:
        copy.start()

    for copy in copies4:
        copy.wait_recv()
    lat_join(recv4, send4)
    for h2 in range(PAIRS):
        cells = base[h2] + lon_join(h2)
        chunk, row = h2 // 4, (h2 % 4) * 2
        flat = obuf.at[chunk].reshape(C * 8, W)
        for p in range(2):
            flat[pl.ds(row + p, C, stride=8), :] = cells[64 * p:64 * p + 64]
        if h2 % 4 == 3:
            store = pltpu.make_async_copy(
                obuf.at[chunk], out_field.at[:, pl.ds(8 * chunk, 8), :], ostore_sem.at[chunk]
            )
            store.start()
            stores.append(store)
        if h2 == 7:
            for copy in reduce3:
                copy.wait_recv()
            red4[pl.ds(pl.multiple_of(8 * k_at, 8), 8), :] = total8(red3)
            reduce4 = reduce_copies(3, [(tile(red4, k_at), tile(red4, k_at))] * 7, k_ids)
            for copy in reduce4:
                copy.start()

    for copy in reduce4:
        copy.wait_recv()
    gpbuf2 = red4[...]
    gbbuf[...] = gpbuf2.T[C:C + 1, :]
    red_out = gpbuf2[:, :C]
    wpbuf[...] = red_out
    last = [
        pltpu.make_async_copy(wpbuf, out_gp, store_sem.at[2]),
        pltpu.make_async_copy(gbbuf, out_gb, store_sem.at[3]),
    ]
    for store in last:
        store.start()
    for store in stores + last:
        store.wait()
    for copy in copies1 + copies2 + copies3 + copies4 + reduce1 + reduce2 + reduce3 + reduce4:
        copy.wait_send()


def body(field, cotangent, w_approx, w_detail, w_point, bias):
    lat_tab, split_tab, join_tab = tables()
    wa = jnp.transpose(w_approx, (0, 2, 3, 1)).reshape(C, 16, C)
    wd = jnp.transpose(w_detail, (0, 1, 3, 4, 2)).reshape(3, C, 16, C)
    anywhere = pl.BlockSpec(memory_space=pl.ANY)
    vmem = pltpu.VMEM
    block = (32, 128)
    gfield, ga, gd, gp, gb = pl.pallas_call(
        kernel,
        out_shape=(
            jax.ShapeDtypeStruct((C, H, W), F32),
            jax.ShapeDtypeStruct((C, 16, C), F32),
            jax.ShapeDtypeStruct((3, C, 16, C), F32),
            jax.ShapeDtypeStruct((C, C), F32),
            jax.ShapeDtypeStruct((1, C), F32),
        ),
        in_specs=[anywhere] * 9,
        out_specs=(anywhere,) * 5,
        scratch_shapes=[
            vmem((4, C, 8, W), F32),
            vmem((4, C, 8, W), F32),
            vmem((4, C, 16, C), F32),
            vmem((C, C), F32),
            vmem((1, C), F32),
            vmem((PAIRS * 16, 2 * C), F32),
            vmem((64, 2 * W), F32),
            vmem((96, W), F32),
            vmem((3 * C, C), BF16),
            vmem((3 * C, C), BF16),
            vmem((PAIRS, 2 * C, W), F32),
            vmem((PAIRS, 2 * C, W), F32),
            vmem((PAIRS * 2 * C, 2 * W), BF16),
            vmem((PAIRS * 2 * C, 2 * W), BF16),
            vmem((PAIRS, 32, 2 * C), F32),
            vmem((16, 32, 2 * C), F32),
            vmem((8,) + block, F32),
            vmem(block, F32),
            vmem((8,) + block, F32),
            vmem(block, F32),
            vmem((8,) + block, F32),
            vmem((8,) + block, F32),
            vmem((8,) + block, F32),
            vmem((8,) + block, F32),
            vmem(block, F32),
            vmem((4, C, 16, C), F32),
            vmem((4, C, 8, W), F32),
            vmem((C, 128), F32),
            vmem((1, C), F32),
            vmem((C, 128), F32),
            vmem((C, 128), F32),
            vmem((C, 128), F32),
            vmem((C, 128), F32),
            pltpu.SemaphoreType.DMA((7,)),
            pltpu.SemaphoreType.DMA((8,)),
            pltpu.SemaphoreType.DMA((4,)),
            pltpu.SemaphoreType.DMA((4,)),
            pltpu.SemaphoreType.DMA((4, 7)),
            pltpu.SemaphoreType.DMA((4, 7)),
            pltpu.SemaphoreType.DMA((4, 7)),
            pltpu.SemaphoreType.DMA((4, 7)),
        ],
        compiler_params=pltpu.CompilerParams(
            collective_id=0, has_side_effects=True, vmem_limit_bytes=48 * 1024 * 1024
        ),
    )(
        field,
        cotangent,
        wa,
        wd,
        w_point,
        bias.reshape(1, C),
        jnp.asarray(lat_tab),
        jnp.asarray(split_tab),
        jnp.asarray(join_tab),
    )
    ga = jnp.transpose(ga.reshape(C, 2, 8, C), (0, 3, 1, 2))
    gd = jnp.transpose(gd.reshape(3, C, 2, 8, C), (0, 1, 4, 2, 3))
    return gfield, ga, gd, gp, gb.reshape(C)


def solution(mesh):
    placed = (
        P(None, "lat", "lon"),
        P(None, "lat", "lon"),
        P(None, None, "lat", "lon"),
        P(None, None, None, "lat", "lon"),
        P(),
        P(),
    )
    return jax.shard_map(
        body,
        mesh=mesh,
        in_specs=placed,
        out_specs=(
            P(None, "lat", "lon"),
            P(None, None, "lat", "lon"),
            P(None, None, None, "lat", "lon"),
            P(),
            P(),
        ),
        check_vma=False,
    )
```

```python
import math

import numpy as np

import jax
import jax.numpy as jnp
from jax import lax
from jax.experimental import pallas as pl
from jax.experimental.pallas import tpu as pltpu
from jax.sharding import PartitionSpec as P

LOW = np.array(
    [
        0.23037781330885523,
        0.7148465705525415,
        0.6308807679295904,
        -0.02798376941698385,
        -0.18703481171888114,
        0.030841381835986965,
        0.032883011666982945,
        -0.010597401784997278,
    ],
    np.float64,
)
HIGH = np.array([LOW[7 - j] if j % 2 == 0 else -LOW[7 - j] for j in range(8)])

C = 64
H = 32
W = 128
LAT = 32
LON = 16
PAIRS = H // 2
F32 = jnp.float32
BF16 = jnp.bfloat16
MESH = pl.DeviceIdType.MESH


def long_filters():
    def spread(taps, step):
        out = np.zeros((len(taps) - 1) * step + 1)
        out[::step] = taps
        return out

    third = np.ones(1)
    for level in range(3):
        third = np.convolve(third, spread(LOW, 2**level))
    return [np.convolve(third, spread(LOW, 8)), np.convolve(third, spread(HIGH, 8))]


def tap(taps, at):
    return taps[at] if 0 <= at < len(taps) else 0.0


def tables():
    both = long_filters()
    lat = np.zeros((PAIRS, 4, 2, 2, 2, C))
    for h2 in range(PAIRS):
        for dl in range(4):
            for u in range(2):
                for ii in range(2):
                    for p in range(2):
                        lat[h2, dl, u, ii, p, :] = tap(both[u], 2 * h2 + p + 32 * dl - 16 * ii)
    lat = lat.reshape(PAIRS * 16, 2 * C).astype(np.float32)
    lon = np.zeros((2, 2, 8, W))
    for ds in range(2):
        for v in range(2):
            for jj in range(8):
                for w in range(W):
                    lon[ds, v, jj, w] = tap(both[v], w + 128 * ds - 16 * jj)
    lon = lon.reshape(32, W).astype(np.float32)
    high = lon.astype(jnp.bfloat16).astype(np.float32)
    rest = (lon - high).astype(jnp.bfloat16).astype(np.float32)
    split = np.concatenate(
        [np.concatenate([high, high], 1), np.concatenate([rest, np.zeros_like(rest)], 1)], 0
    )
    join = np.concatenate([high, rest, high], 0)
    return lat, split, join


def halves(x):
    high = x.astype(BF16)
    return high, (x - high.astype(F32)).astype(BF16)


def swap(x):
    return pltpu.roll(x, 64, axis=1)


def dot_nt(a, b):
    return lax.dot_general(a, b, (((1,), (1,)), ((), ())), preferred_element_type=F32)


def dot_tn(a, b):
    return lax.dot_general(a, b, (((0,), (0,)), ((), ())), preferred_element_type=F32)


def gelu_slope(p):
    cdf = 0.5 * (1.0 + lax.erf(p * (1.0 / math.sqrt(2.0))))
    pdf = jnp.exp(-0.5 * p * p) * (1.0 / math.sqrt(2.0 * math.pi))
    return cdf + p * pdf


def lat_join(recv, own, dup, left):
    for dl in range(4):
        blocks = [own[...] if (dl, ds) == (0, 0) else recv[dl * 2 + ds] for ds in range(2)]
        for u in range(2):
            rows = jnp.concatenate([b[u * 16:(u + 1) * 16] for b in blocks], 0)
            turned = swap(rows)
            dup[dl * 4 + u * 2] = jnp.where(left, rows, turned)
            dup[dl * 4 + u * 2 + 1] = jnp.where(left, turned, rows)


def lon_join(h2, dup, lat_tab, join_tab):
    total = jnp.zeros((32, 2 * C), F32)
    for m in range(16):
        total = total + lat_tab[pl.ds(h2 * 16 + m, 1), :] * dup[m]
    high, rest = halves(total)
    return dot_tn(jnp.concatenate([high, high, rest], 0), join_tab[...].astype(BF16))


def kernel(
    field, cot, wa, wd, wpoint, bias, lat_hbm, split_hbm, join_hbm,
    base, recv4, send4, out_gw, out_gp, out_gb, lat_tab, join_tab,
    fbuf, cbuf, wbuf, wpbuf, biasbuf, split_tab,
    wfwd, wbwd, grad, thl, ghl, yscr, dup,
    send1, send2, send3, recv1, recv2, recv3, coarse,
    red1, red2, red3, red4, red5,
    load_sem, fload_sem, send_sem, recv_sem, rsend_sem, rrecv_sem,
):
    lat_at = lax.axis_index("lat")
    lon_at = lax.axis_index("lon")
    left = lax.broadcasted_iota(jnp.int32, (32, 2 * C), 1) < C

    steps = [(0, 1), (1, 1), (2, 1), (3, 1), (3, 0), (2, 0), (1, 0)]
    behind = [(lax.rem(lat_at + (LAT - dl), LAT), lax.rem(lon_at + (LON - ds), LON)) for dl, ds in steps]
    ahead = [(lax.rem(lat_at + dl, LAT), lax.rem(lon_at + ds, LON)) for dl, ds in steps]
    zhi = lon_at // 8
    x_at = lax.rem(lon_at, 8) // 2
    core = lax.rem(lon_at, 2)
    y_at = lax.rem(lat_at, 4)
    zlo = lat_at // 4
    run, inner = zhi * 2 + zlo // 4, lax.rem(zlo, 4)

    def at(z_run, z_inner):
        return (lax.rem(z_run, 2) * 16 + z_inner * 4 + y_at, (z_run // 2) * 8 + lax.rem(lon_at, 8))

    turns = [lambda i, d=d: lax.rem(i + d, 4) for d in (2, 1, 3)]
    sum_steps = [
        (core, [(lat_at, lon_at + 1 - 2 * core)]),
        (y_at, [(zlo * 4 + t(y_at), lon_at) for t in turns]),
        (x_at, [(lat_at, zhi * 8 + t(x_at) * 2 + core) for t in turns]),
        (inner, [at(run, t(inner)) for t in turns]),
        (run, [at(t(run), inner) for t in turns]),
    ]

    barrier = pltpu.get_barrier_semaphore()
    everyone = sum_steps[4][1] + behind + ahead + sum_steps[3][1] + sum_steps[2][1]

    field_loads = [
        pltpu.make_async_copy(field.at[:, pl.ds(8 * q, 8), :], fbuf.at[q], fload_sem.at[q]) for q in range(4)
    ]
    for load in field_loads:
        load.start()
    split_load = pltpu.make_async_copy(split_hbm, split_tab, load_sem.at[0])
    lat_load = pltpu.make_async_copy(lat_hbm, lat_tab, load_sem.at[1])
    wp_load = pltpu.make_async_copy(wpoint, wpbuf, load_sem.at[2])
    bias_load = pltpu.make_async_copy(bias, biasbuf, load_sem.at[3])
    wa_load = pltpu.make_async_copy(wa, wbuf.at[0], load_sem.at[4])
    wd_load = pltpu.make_async_copy(wd, wbuf.at[pl.ds(1, 3)], load_sem.at[5])
    cot_loads = [
        pltpu.make_async_copy(cot.at[:, pl.ds(8 * q, 8), :], cbuf.at[q], fload_sem.at[4 + q]) for q in range(4)
    ]
    join_load = pltpu.make_async_copy(join_hbm, join_tab, load_sem.at[6])
    for load in [split_load, lat_load, wp_load, bias_load, wa_load, wd_load, join_load] + cot_loads:
        load.start()
    for device in everyone:
        pl.semaphore_signal(barrier, inc=1, device_id=device, device_id_type=MESH)

    def cell_pair(buffer, h2):
        chunk, row = h2 // 4, (h2 % 4) * 2
        flat = buffer.at[chunk].reshape(C * 8, W)
        return jnp.concatenate([flat[pl.ds(row + p, C, stride=8), :] for p in range(2)], 0)

    def lon_split(rows, at):
        both = dot_nt(split_tab[...].astype(BF16), rows)
        sums = both[:32] + both[32:]
        yscr[at, :, :] = sums[:, :128]
        yscr[at + 1, :, :] = sums[:, 128:]

    def lat_split(buffer, on_block):
        for dl in (3, 2, 1, 0):
            def step(g, sums, dl=dl):
                sums = list(sums)
                for n in range(4):
                    h2 = g * 4 + n
                    y = yscr[h2]
                    for m in range(4):
                        sums[m] = sums[m] + lat_tab[pl.ds(h2 * 16 + dl * 4 + m, 1), :] * y
                return tuple(sums)

            zero = jnp.zeros((32, 2 * C), F32)
            sums = lax.fori_loop(0, 4, step, (zero,) * 4)
            for u in range(2):
                first, second = sums[2 * u], sums[2 * u + 1]
                modes = jnp.where(left, first, second) + swap(jnp.where(left, second, first))
                for ds in range(2):
                    buffer[dl * 2 + ds, u * 16:(u + 1) * 16, :] = modes[ds * 16:(ds + 1) * 16]
            on_block(dl)

    def exchange(number, source_of, recv, targets):
        return [
            pltpu.make_async_remote_copy(
                src_ref=source_of(dl * 2 + ds),
                dst_ref=recv.at[dl * 2 + ds],
                send_sem=send_sem.at[number, n],
                recv_sem=recv_sem.at[number, n],
                device_id=targets[n],
                device_id_type=MESH,
            )
            for n, (dl, ds) in enumerate(steps)
        ]

    def start_block(copies):
        def on_block(dl):
            for n, step in enumerate(steps):
                if step[0] == dl:
                    copies[n].start()
        return on_block

    def point_map(weights, rows):
        high = [rows[64 * n:64 * n + 64, :W] for n in range(4)]
        rest = [rows[64 * n:64 * n + 64, W:] for n in range(4)]
        high = jnp.concatenate(high, 1)
        rest = jnp.concatenate(rest, 1)
        out = dot_tn(weights, jnp.concatenate([high, rest, high], 0))
        return jnp.concatenate([out[:, W * n:W * n + W] for n in range(4)], 0)

    split_load.wait()
    for q in range(4):
        field_loads[q].wait()
        for n in range(2):
            h2 = q * 4 + n * 2
            for k in range(2):
                high, rest = halves(cell_pair(fbuf, h2 + k))
                thl[(h2 + k) * 128:(h2 + k + 1) * 128, :W] = high
                thl[(h2 + k) * 128:(h2 + k + 1) * 128, W:] = rest
            lon_split(thl[h2 * 128:h2 * 128 + 256, :], h2)
    lat_load.wait()
    pl.semaphore_wait(barrier, len(everyone))
    copies1 = exchange(0, lambda n: send1.at[n], recv1, behind)
    lat_split(send1, start_block(copies1))

    wp_load.wait()
    bias_load.wait()
    high, rest = halves(wpbuf[...])
    wbwd[...] = jnp.concatenate([high, high, rest], 0)
    high, rest = halves(wpbuf[...].T)
    wfwd[...] = jnp.concatenate([high, high, rest], 0)
    bias_cells = jnp.broadcast_to(biasbuf[...], (W, C)).T
    bias_cells = jnp.concatenate([bias_cells, bias_cells], 0)
    for h4 in range(PAIRS // 2):
        mapped = point_map(wfwd[...], thl[h4 * 256:h4 * 256 + 256, :])
        for k in range(2):
            h2 = 2 * h4 + k
            base[h2] = mapped[128 * k:128 * k + 128] + cell_pair(fbuf, h2) + bias_cells
    wa_load.wait()
    wd_load.wait()

    total = send1[0]
    for n, (dl, ds) in enumerate(steps):
        copies1[n].wait_recv()
        total = total + recv1[dl * 2 + ds]
    coarse[...] = total

    def mix(g, carry):
        turned, sums = carry
        sums = list(sums)
        for k in range(8):
            for b in range(4):
                rows = turned[8 * b:8 * b + 8]
                column = jnp.concatenate([rows[:, k:k + 1], rows[:, C + k:C + k + 1]], 0)
                sums[b] = sums[b] + column * wbuf[b, g * 8 + k]
        return pltpu.roll(turned, 2 * C - 8, axis=1), tuple(sums)

    def packed(parts):
        return jnp.concatenate([jnp.concatenate([p[:8], p[8:]], 1) for p in parts], 0)

    _, mixed = lax.fori_loop(0, C // 8, mix, (total, (jnp.zeros((16, C), F32),) * 4))
    send2[...] = packed(mixed) - total
    copies2 = exchange(1, lambda n: send2, recv2, ahead)
    for copy in copies2:
        copy.start()

    join_load.wait()
    for load in cot_loads:
        load.wait()
    for copy in copies2:
        copy.wait_recv()
    lat_join(recv2, send2, dup, left)

    for h4 in range(PAIRS // 2):
        for k in range(2):
            h2 = 2 * h4 + k
            g = gelu_slope(base[h2] + lon_join(h2, dup, lat_tab, join_tab)) * cell_pair(cbuf, h2)
            grad[h2] = g
            high, rest = halves(g)
            ghl[h2 * 128:(h2 + 1) * 128, :W] = high
            ghl[h2 * 128:(h2 + 1) * 128, W:] = rest
        lon_split(ghl[h4 * 256:h4 * 256 + 256, :], 2 * h4)
    copies3 = exchange(2, lambda n: send3.at[n], recv3, behind)
    lat_split(send3, start_block(copies3))

    point = jnp.zeros((128, 128), F32)
    rows_sum = jnp.zeros((C, W), F32)
    for h2 in range(PAIRS):
        at = h2 * 128
        both = []
        for source in (ghl, thl):
            tops = jnp.concatenate([source[at:at + 64, :W], source[at + 64:at + 128, :W]], 1)
            rests = jnp.concatenate([source[at:at + 64, W:], source[at + 64:at + 128, W:]], 1)
            both.append(jnp.concatenate([tops, rests], 0))
        point = point + dot_nt(both[0], both[1])
        rows_sum = rows_sum + grad[h2, 0:64, :] + grad[h2, 64:128, :]
    point = point[:C] + point[C:]
    point = point + swap(point)
    bias_term = jnp.sum(rows_sum, axis=1, keepdims=True)
    sums_of = [red1, red2, red3, red4, red5]
    folded = jnp.concatenate([point[: C // 2, :C], point[C // 2:, :C]], 1)
    bias_row = jnp.broadcast_to(bias_term, (C, 128)).T[:8]
    first = jnp.concatenate([folded, jnp.concatenate([bias_row, bias_row], 1)], 0)
    reduces = []

    def send_sum(number, rows):
        own, ids = sum_steps[number]
        ref = sums_of[number]
        ref[pl.ds(own, 1)] = rows[None]
        copies = [
            pltpu.make_async_remote_copy(
                src_ref=ref.at[own],
                dst_ref=ref.at[own],
                send_sem=rsend_sem.at[number, n],
                recv_sem=rrecv_sem.at[number, n],
                device_id=device,
                device_id_type=MESH,
            )
            for n, device in enumerate(ids)
        ]
        for copy in copies:
            copy.start()
        reduces.append(copies)

    def take_sum(number):
        for copy in reduces[number]:
            copy.wait_recv()
        ref = sums_of[number]
        rows = ref[0]
        for n in range(1, len(reduces[number]) + 1):
            rows = rows + ref[n]
        return rows

    send_sum(0, first)

    for h4 in range(PAIRS // 2):
        mapped = point_map(wbwd[...], ghl[h4 * 256:h4 * 256 + 256, :])
        for k in range(2):
            h2 = 2 * h4 + k
            base[h2] = mapped[128 * k:128 * k + 128] + grad[h2]
    send_sum(1, take_sum(0))
    send_sum(2, take_sum(1))
    send_sum(3, take_sum(2))

    gtotal = send3[0]
    for n, (dl, ds) in enumerate(steps):
        copies3[n].wait_recv()
        gtotal = gtotal + recv3[dl * 2 + ds]

    def unpacked(rows, b):
        part = rows[8 * b:8 * b + 8]
        return jnp.concatenate([part[:, :C], part[:, C:]], 0)

    gmodes = [unpacked(gtotal, b) for b in range(4)]
    lanes16 = lax.broadcasted_iota(jnp.int32, (16, C), 1)

    def back(g, sums):
        sums = list(sums)
        for k in range(8):
            for b in range(4):
                one = jnp.sum(wbuf[b, g * 8 + k] * gmodes[b], axis=1, keepdims=True)
                sums[b] = jnp.where(lanes16 == g * 8 + k, one, sums[b])
        return tuple(sums)

    backs = lax.fori_loop(0, C // 8, back, (jnp.zeros((16, C), F32),) * 4)
    send4[...] = packed(backs) - gtotal
    copies4 = exchange(3, lambda n: send4, recv4, ahead)
    for copy in copies4:
        copy.start()

    send_sum(4, take_sum(3))

    def outer(g, turned):
        for k in range(8):
            for b in range(4):
                rows = turned[8 * b:8 * b + 8]
                column = jnp.concatenate([rows[:, k:k + 1], rows[:, C + k:C + k + 1]], 0)
                out_gw[b, g * 8 + k] = column * gmodes[b]
        return pltpu.roll(turned, 2 * C - 8, axis=1)

    lax.fori_loop(0, C // 8, outer, coarse[...])
    for copy in copies4:
        copy.wait_recv()
    rows = take_sum(4)
    out_gp[...] = jnp.concatenate([rows[: C // 2, :C], rows[: C // 2, C:]], 0)
    out_gb[...] = rows[C // 2:C // 2 + 1, :C]
    for copy in copies1 + copies2 + copies3 + copies4 + sum(reduces, []):
        copy.wait_send()


def last_kernel(
    base, recv4, send4, gw, gp, gb, lat_tab, join_tab, out_field, out_ga, out_gd, out_gp, out_gb, dup, obuf, sem
):
    stores = []

    def store(src, dst):
        stores.append(pltpu.make_async_copy(src, dst, sem.at[len(stores)]))
        stores[-1].start()

    store(gw.at[0], out_ga)
    for b in range(3):
        store(gw.at[1 + b], out_gd.at[b])
    store(gp, out_gp)
    store(gb, out_gb)
    left = lax.broadcasted_iota(jnp.int32, (32, 2 * C), 1) < C
    lat_join(recv4, send4, dup, left)
    for h2 in range(PAIRS):
        cells = base[h2] + lon_join(h2, dup, lat_tab, join_tab)
        chunk, row = h2 // 4, (h2 % 4) * 2
        flat = obuf.at[chunk].reshape(C * 8, W)
        for p in range(2):
            flat[pl.ds(row + p, C, stride=8), :] = cells[64 * p:64 * p + 64]
        if h2 % 4 == 3:
            store(obuf.at[chunk], out_field.at[:, pl.ds(8 * chunk, 8), :])
    for copy in stores:
        copy.wait()


def body(field, cotangent, w_approx, w_detail, w_point, bias):
    lat_tab, split_tab, join_tab = tables()
    wa = jnp.transpose(w_approx, (0, 2, 3, 1)).reshape(C, 16, C)
    wd = jnp.transpose(w_detail, (0, 1, 3, 4, 2)).reshape(3, C, 16, C)
    anywhere = pl.BlockSpec(memory_space=pl.ANY)
    vmem = pltpu.VMEM
    block = (32, 128)
    hbm = pl.BlockSpec(memory_space=pltpu.HBM)
    results = pl.pallas_call(
        kernel,
        out_shape=(
            vmem((PAIRS, 2 * C, W), F32),
            vmem((8,) + block, F32),
            vmem(block, F32),
            vmem((4, C, 16, C), F32),
            vmem((C, C), F32),
            vmem((1, C), F32),
            vmem((PAIRS * 16, 2 * C), F32),
            vmem((96, W), F32),
        ),
        in_specs=[hbm] * 9,
        out_specs=(pl.BlockSpec(memory_space=vmem),) * 8,
        scratch_shapes=[
            vmem((4, C, 8, W), F32),
            vmem((4, C, 8, W), F32),
            vmem((4, C, 16, C), F32),
            vmem((C, C), F32),
            vmem((1, C), F32),
            vmem((64, 2 * W), F32),
            vmem((3 * C, C), BF16),
            vmem((3 * C, C), BF16),
            vmem((PAIRS, 2 * C, W), F32),
            vmem((PAIRS * 2 * C, 2 * W), BF16),
            vmem((PAIRS * 2 * C, 2 * W), BF16),
            vmem((PAIRS, 32, 2 * C), F32),
            vmem((16, 32, 2 * C), F32),
            vmem((8,) + block, F32),
            vmem(block, F32),
            vmem((8,) + block, F32),
            vmem((8,) + block, F32),
            vmem((8,) + block, F32),
            vmem((8,) + block, F32),
            vmem(block, F32),
            vmem((2, 40, 128), F32),
            vmem((4, 40, 128), F32),
            vmem((4, 40, 128), F32),
            vmem((4, 40, 128), F32),
            vmem((4, 40, 128), F32),
            pltpu.SemaphoreType.DMA((7,)),
            pltpu.SemaphoreType.DMA((8,)),
            pltpu.SemaphoreType.DMA((4, 7)),
            pltpu.SemaphoreType.DMA((4, 7)),
            pltpu.SemaphoreType.DMA((5, 3)),
            pltpu.SemaphoreType.DMA((5, 3)),
        ],
        compiler_params=pltpu.CompilerParams(
            collective_id=0, has_side_effects=True, vmem_limit_bytes=48 * 1024 * 1024
        ),
    )(
        *[
            pltpu.with_memory_space_constraint(x, pltpu.HBM)
            for x in (
                field,
                cotangent,
                wa,
                wd,
                w_point,
                bias.reshape(1, C),
                jnp.asarray(lat_tab),
                jnp.asarray(split_tab),
                jnp.asarray(join_tab),
            )
        ]
    )
    gfield, ga, gd, gp, gb = pl.pallas_call(
        last_kernel,
        out_shape=(
            jax.ShapeDtypeStruct((C, H, W), F32),
            jax.ShapeDtypeStruct((C, 16, C), F32),
            jax.ShapeDtypeStruct((3, C, 16, C), F32),
            jax.ShapeDtypeStruct((C, C), F32),
            jax.ShapeDtypeStruct((1, C), F32),
        ),
        in_specs=[pl.BlockSpec(memory_space=vmem)] * 8,
        out_specs=(anywhere,) * 5,
        scratch_shapes=[
            vmem((16, 32, 2 * C), F32),
            vmem((4, C, 8, W), F32),
            pltpu.SemaphoreType.DMA((10,)),
        ],
        compiler_params=pltpu.CompilerParams(vmem_limit_bytes=32 * 1024 * 1024),
    )(*[pltpu.with_memory_space_constraint(x, vmem) for x in results])
    ga = jnp.transpose(ga.reshape(C, 2, 8, C), (0, 3, 1, 2))
    gd = jnp.transpose(gd.reshape(3, C, 2, 8, C), (0, 1, 4, 2, 3))
    return gfield, ga, gd, gp, gb.reshape(C)


def solution(mesh):
    placed = (
        P(None, "lat", "lon"),
        P(None, "lat", "lon"),
        P(None, None, "lat", "lon"),
        P(None, None, None, "lat", "lon"),
        P(),
        P(),
    )
    return jax.shard_map(
        body,
        mesh=mesh,
        in_specs=placed,
        out_specs=(
            P(None, "lat", "lon"),
            P(None, None, "lat", "lon"),
            P(None, None, None, "lat", "lon"),
            P(),
            P(),
        ),
        check_vma=False,
    )
```

```python
import math

import numpy as np

import jax
import jax.numpy as jnp
from jax import lax
from jax.experimental import pallas as pl
from jax.experimental.pallas import tpu as pltpu
from jax.sharding import PartitionSpec as P

LOW = np.array(
    [
        0.23037781330885523,
        0.7148465705525415,
        0.6308807679295904,
        -0.02798376941698385,
        -0.18703481171888114,
        0.030841381835986965,
        0.032883011666982945,
        -0.010597401784997278,
    ],
    np.float64,
)
HIGH = np.array([LOW[7 - j] if j % 2 == 0 else -LOW[7 - j] for j in range(8)])

C = 64
H = 32
W = 128
LAT = 32
LON = 16
PAIRS = H // 2
F32 = jnp.float32
BF16 = jnp.bfloat16
MESH = pl.DeviceIdType.MESH


def long_filters():
    def spread(taps, step):
        out = np.zeros((len(taps) - 1) * step + 1)
        out[::step] = taps
        return out

    third = np.ones(1)
    for level in range(3):
        third = np.convolve(third, spread(LOW, 2**level))
    return [np.convolve(third, spread(LOW, 8)), np.convolve(third, spread(HIGH, 8))]


def tap(taps, at):
    return taps[at] if 0 <= at < len(taps) else 0.0


def tables():
    both = long_filters()
    lat = np.zeros((PAIRS, 4, 2, 2, 2, C))
    for h2 in range(PAIRS):
        for dl in range(4):
            for u in range(2):
                for ii in range(2):
                    for p in range(2):
                        lat[h2, dl, u, ii, p, :] = tap(both[u], 2 * h2 + p + 32 * dl - 16 * ii)
    lat = lat.reshape(PAIRS * 16, 2 * C).astype(np.float32)
    lon = np.zeros((2, 2, 8, W))
    for ds in range(2):
        for v in range(2):
            for jj in range(8):
                for w in range(W):
                    lon[ds, v, jj, w] = tap(both[v], w + 128 * ds - 16 * jj)
    lon = lon.reshape(32, W).astype(np.float32)
    high = lon.astype(jnp.bfloat16).astype(np.float32)
    rest = (lon - high).astype(jnp.bfloat16).astype(np.float32)
    split = np.concatenate(
        [np.concatenate([high, high], 1), np.concatenate([rest, np.zeros_like(rest)], 1)], 0
    )
    join = np.concatenate([high, rest, high], 0)
    return lat, split, join


USED = (tables()[0].reshape(PAIRS, 4, 4, 2 * C) != 0).any(axis=3).tolist()


def halves(x):
    high = x.astype(BF16)
    return high, (x - high.astype(F32)).astype(BF16)


def swap(x):
    return pltpu.roll(x, 64, axis=1)


def dot_nt(a, b):
    return lax.dot_general(a, b, (((1,), (1,)), ((), ())), preferred_element_type=F32)


def dot_tn(a, b):
    return lax.dot_general(a, b, (((0,), (0,)), ((), ())), preferred_element_type=F32)


def gelu_slope(p):
    cdf = 0.5 * (1.0 + lax.erf(p * (1.0 / math.sqrt(2.0))))
    pdf = jnp.exp(-0.5 * p * p) * (1.0 / math.sqrt(2.0 * math.pi))
    return cdf + p * pdf


def lat_join(recv, own, dup, left):
    for dl in range(4):
        blocks = [own[...] if (dl, ds) == (0, 0) else recv[dl * 2 + ds] for ds in range(2)]
        for u in range(2):
            rows = jnp.concatenate([b[u * 16:(u + 1) * 16] for b in blocks], 0)
            turned = swap(rows)
            dup[dl * 4 + u * 2] = jnp.where(left, rows, turned)
            dup[dl * 4 + u * 2 + 1] = jnp.where(left, turned, rows)


def lon_join(h2, dup, lat_tab, join_tab):
    total = jnp.zeros((32, 2 * C), F32)
    for m in range(16):
        total = total + lat_tab[pl.ds(h2 * 16 + m, 1), :] * dup[m]
    high, rest = halves(total)
    return dot_tn(jnp.concatenate([high, high, rest], 0), join_tab[...].astype(BF16))


def kernel(
    field, cot, wa, wd, wpoint, bias, lat_hbm, split_hbm, join_hbm,
    base, recv4, send4, out_gw, out_gp, out_gb, lat_tab, join_tab,
    fbuf, cbuf, wbuf, wpbuf, biasbuf, split_tab,
    wmix, wfwd, wbwd, grad, thl, ghl, yscr, dup,
    send1, send2, send3, recv1, recv2, recv3, coarse,
    red1, red2, red3, red4,
    load_sem, fload_sem, send_sem, recv_sem, rsend_sem, rrecv_sem,
):
    lat_at = lax.axis_index("lat")
    lon_at = lax.axis_index("lon")
    left = lax.broadcasted_iota(jnp.int32, (32, 2 * C), 1) < C

    steps = [(2, 1), (1, 1), (3, 1), (0, 1), (2, 0), (1, 0), (3, 0)]
    behind = [(lax.rem(lat_at + (LAT - dl), LAT), lax.rem(lon_at + (LON - ds), LON)) for dl, ds in steps]
    ahead = [(lax.rem(lat_at + dl, LAT), lax.rem(lon_at + ds, LON)) for dl, ds in steps]
    zhi = lon_at // 8
    x_at = lax.rem(lon_at, 8) // 2
    core = lax.rem(lon_at, 2)
    y_at = lax.rem(lat_at, 4)
    zlo = lat_at // 4
    run, inner = zhi * 2 + zlo // 4, lax.rem(zlo, 4)

    def at(z_run, z_inner):
        return (lax.rem(z_run, 2) * 16 + z_inner * 4 + y_at, (z_run // 2) * 8 + lax.rem(lon_at, 8))

    turns = [lambda i, d=d: lax.rem(i + d, 4) for d in (2, 1, 3)]
    same_core = [(zlo * 4 + t(y_at), lon_at) for t in turns]
    other_core = [(zlo * 4 + t(y_at), lon_at + 1 - 2 * core) for t in turns]
    sum_steps = [
        (core * 4 + y_at, same_core + other_core + [(lat_at, lon_at + 1 - 2 * core)]),
        (x_at, [(lat_at, zhi * 8 + t(x_at) * 2 + core) for t in turns]),
        (inner, [at(run, t(inner)) for t in turns]),
        (run, [at(t(run), inner) for t in turns]),
    ]

    barrier = pltpu.get_barrier_semaphore()
    everyone = sum_steps[3][1] + behind + ahead + sum_steps[2][1] + sum_steps[1][1] + other_core

    field_loads = [
        pltpu.make_async_copy(field.at[:, pl.ds(8 * q, 8), :], fbuf.at[q], fload_sem.at[q]) for q in range(4)
    ]
    for load in field_loads:
        load.start()
    split_load = pltpu.make_async_copy(split_hbm, split_tab, load_sem.at[0])
    lat_load = pltpu.make_async_copy(lat_hbm, lat_tab, load_sem.at[1])
    wp_load = pltpu.make_async_copy(wpoint, wpbuf, load_sem.at[2])
    bias_load = pltpu.make_async_copy(bias, biasbuf, load_sem.at[3])
    wa_load = pltpu.make_async_copy(wa, wbuf.at[0], load_sem.at[4])
    wd_load = pltpu.make_async_copy(wd, wbuf.at[pl.ds(1, 3)], load_sem.at[5])
    cot_loads = [
        pltpu.make_async_copy(cot.at[:, pl.ds(8 * q, 8), :], cbuf.at[q], fload_sem.at[4 + q]) for q in range(4)
    ]
    join_load = pltpu.make_async_copy(join_hbm, join_tab, load_sem.at[6])
    for load in [split_load, lat_load, wp_load, bias_load, wa_load, wd_load, join_load] + cot_loads:
        load.start()
    for device in everyone:
        pl.semaphore_signal(barrier, inc=1, device_id=device, device_id_type=MESH)

    def cell_pair(buffer, h2):
        chunk, row = h2 // 4, (h2 % 4) * 2
        flat = buffer.at[chunk].reshape(C * 8, W)
        return jnp.concatenate([flat[pl.ds(row + p, C, stride=8), :] for p in range(2)], 0)

    def lon_split(rows, at):
        both = dot_nt(split_tab[...].astype(BF16), rows)
        sums = both[:32] + both[32:]
        yscr[at, :, :] = sums[:, :128]
        yscr[at + 1, :, :] = sums[:, 128:]

    def lat_split(buffer, send):
        for dl in (2, 1, 3, 0):
            sums = [None] * 4
            for h2 in range(PAIRS):
                y = yscr[h2]
                for m in range(4):
                    if USED[h2][dl][m]:
                        term = lat_tab[pl.ds(h2 * 16 + dl * 4 + m, 1), :] * y
                        sums[m] = term if sums[m] is None else sums[m] + term
            for u in range(2):
                first, second = sums[2 * u], sums[2 * u + 1]
                modes = jnp.where(left, first, second) + swap(jnp.where(left, second, first))
                for ds in range(2):
                    buffer[dl * 2 + ds, u * 16:(u + 1) * 16, :] = modes[ds * 16:(ds + 1) * 16]
            send(dl, 1)
        for dl in (2, 1, 3):
            send(dl, 0)

    def exchange(number, source_of, recv, targets):
        return [
            pltpu.make_async_remote_copy(
                src_ref=source_of(dl * 2 + ds),
                dst_ref=recv.at[dl * 2 + ds],
                send_sem=send_sem.at[number, n],
                recv_sem=recv_sem.at[number, n],
                device_id=targets[n],
                device_id_type=MESH,
            )
            for n, (dl, ds) in enumerate(steps)
        ]

    def point_map(weights, rows):
        high = [rows[64 * n:64 * n + 64, :W] for n in range(4)]
        rest = [rows[64 * n:64 * n + 64, W:] for n in range(4)]
        high = jnp.concatenate(high, 1)
        rest = jnp.concatenate(rest, 1)
        out = dot_tn(weights, jnp.concatenate([high, rest, high], 0))
        return jnp.concatenate([out[:, W * n:W * n + W] for n in range(4)], 0)

    split_load.wait()
    for q in range(4):
        field_loads[q].wait()
        for n in range(2):
            h2 = q * 4 + n * 2
            for k in range(2):
                high, rest = halves(cell_pair(fbuf, h2 + k))
                thl[(h2 + k) * 128:(h2 + k + 1) * 128, :W] = high
                thl[(h2 + k) * 128:(h2 + k + 1) * 128, W:] = rest
            lon_split(thl[h2 * 128:h2 * 128 + 256, :], h2)
    lat_load.wait()
    lat_split(send1, lambda dl, ds: None)
    pl.semaphore_wait(barrier, len(everyone))
    copies1 = exchange(0, lambda n: send1.at[n], recv1, behind)
    for copy in copies1:
        copy.start()

    wp_load.wait()
    bias_load.wait()
    high, rest = halves(wpbuf[...])
    wbwd[...] = jnp.concatenate([high, high, rest], 0)
    high, rest = halves(wpbuf[...].T)
    wfwd[...] = jnp.concatenate([high, high, rest], 0)
    bias_cells = jnp.broadcast_to(biasbuf[...], (W, C)).T
    bias_cells = jnp.concatenate([bias_cells, bias_cells], 0)
    for h4 in range(PAIRS // 2):
        mapped = point_map(wfwd[...], thl[h4 * 256:h4 * 256 + 256, :])
        for k in range(2):
            h2 = 2 * h4 + k
            base[h2] = mapped[128 * k:128 * k + 128] + cell_pair(fbuf, h2) + bias_cells
    wa_load.wait()
    wd_load.wait()

    def prepare(b, carry):
        flat = wbuf.at[b].reshape(C * 16, C)
        for n in range(16):
            one = flat[pl.ds(n, C, stride=16), :]
            high = one.astype(BF16).astype(F32)
            wmix[b * 16 + n] = jnp.concatenate([high, one - high], 1).astype(BF16)
        return carry

    lax.fori_loop(0, 4, prepare, 0)

    total = send1[0]
    for n, (dl, ds) in enumerate(steps):
        copies1[n].wait_recv()
        total = total + recv1[dl * 2 + ds]
    coarse[...] = total

    row8 = lax.broadcasted_iota(jnp.int32, (8, 2 * C), 0)
    half8 = lax.broadcasted_iota(jnp.int32, (8, 2 * C), 1) // C
    left8 = half8 == 0

    def stacked(x):
        high = x.astype(BF16).astype(F32)
        return jnp.concatenate([high, x - high], 0).astype(BF16)

    mixed = []
    for b in range(4):
        both = []
        for ii in range(2):
            rows = total[8 * b:8 * b + 8]
            lhs = stacked((rows if ii == 0 else swap(rows))[:, :C])
            kept = jnp.zeros((8, 2 * C), F32)
            for j2 in range(4):
                at = b * 16 + ii * 8 + j2 * 2
                out = jnp.dot(lhs, jnp.concatenate([wmix[at], wmix[at + 1]], 1), preferred_element_type=F32)
                out = out[:8] + out[8:]
                kept = jnp.where(row8 == 2 * j2, out[:, :128], kept)
                kept = jnp.where(row8 == 2 * j2 + 1, out[:, 128:], kept)
            both.append(kept + swap(kept))
        mixed.append(jnp.where(left8, both[0], both[1]))
    send2[...] = jnp.concatenate(mixed, 0) - total
    copies2 = exchange(1, lambda n: send2, recv2, ahead)
    for copy in copies2:
        copy.start()

    join_load.wait()
    for load in cot_loads:
        load.wait()
    for copy in copies2:
        copy.wait_recv()
    lat_join(recv2, send2, dup, left)

    for h2 in range(PAIRS):
        base[h2] = base[h2] + lon_join(h2, dup, lat_tab, join_tab)
    for h2 in range(PAIRS):
        g = gelu_slope(base[h2]) * cell_pair(cbuf, h2)
        grad[h2] = g
        high, rest = halves(g)
        ghl[h2 * 128:(h2 + 1) * 128, :W] = high
        ghl[h2 * 128:(h2 + 1) * 128, W:] = rest
    for h4 in range(PAIRS // 2):
        lon_split(ghl[h4 * 256:h4 * 256 + 256, :], 2 * h4)
    copies3 = exchange(2, lambda n: send3.at[n], recv3, behind)
    lat_split(send3, lambda dl, ds: copies3[steps.index((dl, ds))].start())

    point = jnp.zeros((128, 128), F32)
    rows_sum = jnp.zeros((C, W), F32)
    for h2 in range(PAIRS):
        at = h2 * 128
        both = []
        for source in (ghl, thl):
            tops = jnp.concatenate([source[at:at + 64, :W], source[at + 64:at + 128, :W]], 1)
            rests = jnp.concatenate([source[at:at + 64, W:], source[at + 64:at + 128, W:]], 1)
            both.append(jnp.concatenate([tops, rests], 0))
        point = point + dot_nt(both[0], both[1])
        rows_sum = rows_sum + grad[h2, 0:64, :] + grad[h2, 64:128, :]
    point = point[:C] + point[C:]
    point = point + swap(point)
    bias_term = jnp.sum(rows_sum, axis=1, keepdims=True)
    sums_of = [red1, red2, red3, red4]
    folded = jnp.concatenate([point[: C // 2, :C], point[C // 2:, :C]], 1)
    bias_row = jnp.broadcast_to(bias_term, (C, 128)).T[:8]
    first = jnp.concatenate([folded, jnp.concatenate([bias_row, bias_row], 1)], 0)
    reduces = []

    def send_sum(number, rows):
        own, ids = sum_steps[number]
        ref = sums_of[number]
        ref[pl.ds(own, 1)] = rows[None]
        copies = [
            pltpu.make_async_remote_copy(
                src_ref=ref.at[own],
                dst_ref=ref.at[own],
                send_sem=rsend_sem.at[number, n],
                recv_sem=rrecv_sem.at[number, n],
                device_id=device,
                device_id_type=MESH,
            )
            for n, device in enumerate(ids)
        ]
        for copy in copies:
            copy.start()
        reduces.append(copies)

    def take_sum(number):
        for copy in reduces[number]:
            copy.wait_recv()
        ref = sums_of[number]
        rows = ref[0]
        for n in range(1, len(reduces[number]) + 1):
            rows = rows + ref[n]
        return rows

    send_sum(0, first)

    for h4 in range(PAIRS // 2):
        mapped = point_map(wbwd[...], ghl[h4 * 256:h4 * 256 + 256, :])
        for k in range(2):
            h2 = 2 * h4 + k
            base[h2] = mapped[128 * k:128 * k + 128] + grad[h2]
    send_sum(1, take_sum(0))
    send_sum(2, take_sum(1))

    gtotal = send3[0]
    for n, (dl, ds) in enumerate(steps):
        copies3[n].wait_recv()
        gtotal = gtotal + recv3[dl * 2 + ds]

    def unpacked(rows, b):
        part = rows[8 * b:8 * b + 8]
        return jnp.concatenate([part[:, :C], part[:, C:]], 0)

    gmodes = [unpacked(gtotal, b) for b in range(4)]
    backs = []
    for b in range(4):
        rows = gtotal[8 * b:8 * b + 8]
        turned = swap(rows)
        both = []
        for ii in range(2):
            lhs = stacked(jnp.where(left8, rows, turned) if ii == 0 else jnp.where(left8, turned, rows))
            maps = wmix[b * 16 + ii * 8:b * 16 + ii * 8 + 8].reshape(8 * C, 2 * C)
            out = dot_nt(lhs, maps)
            out = out[:8] + out[8:]
            kept = jnp.zeros((8, 2 * C), F32)
            for j2 in range(4):
                part = out[:, 128 * j2:128 * j2 + 128]
                kept = jnp.where(row8 - half8 == 2 * j2, part, kept)
            both.append(kept + swap(kept))
        backs.append(jnp.where(left8, both[0], both[1]))
    send4[...] = jnp.concatenate(backs, 0) - gtotal
    copies4 = exchange(3, lambda n: send4, recv4, ahead)
    for copy in copies4:
        copy.start()

    send_sum(3, take_sum(2))

    def outer(g, turned):
        for k in range(8):
            for b in range(4):
                rows = turned[8 * b:8 * b + 8]
                column = jnp.concatenate([rows[:, k:k + 1], rows[:, C + k:C + k + 1]], 0)
                out_gw[b, g * 8 + k] = column * gmodes[b]
        return pltpu.roll(turned, 2 * C - 8, axis=1)

    lax.fori_loop(0, C // 8, outer, coarse[...])
    for copy in copies4:
        copy.wait_recv()
    rows = take_sum(3)
    out_gp[...] = jnp.concatenate([rows[: C // 2, :C], rows[: C // 2, C:]], 0)
    out_gb[...] = rows[C // 2:C // 2 + 1, :C]
    for copy in copies1 + copies2 + copies3 + copies4 + sum(reduces, []):
        copy.wait_send()


def last_kernel(
    base, recv4, send4, gw, gp, gb, lat_tab, join_tab, out_field, out_ga, out_gd, out_gp, out_gb, dup, obuf, sem
):
    stores = []

    def store(src, dst):
        stores.append(pltpu.make_async_copy(src, dst, sem.at[len(stores)]))
        stores[-1].start()

    store(gw.at[0], out_ga)
    for b in range(3):
        store(gw.at[1 + b], out_gd.at[b])
    store(gp, out_gp)
    store(gb, out_gb)
    left = lax.broadcasted_iota(jnp.int32, (32, 2 * C), 1) < C
    lat_join(recv4, send4, dup, left)
    for h2 in range(PAIRS):
        cells = base[h2] + lon_join(h2, dup, lat_tab, join_tab)
        chunk, row = h2 // 4, (h2 % 4) * 2
        flat = obuf.at[chunk].reshape(C * 8, W)
        for p in range(2):
            flat[pl.ds(row + p, C, stride=8), :] = cells[64 * p:64 * p + 64]
        if h2 % 4 == 3:
            store(obuf.at[chunk], out_field.at[:, pl.ds(8 * chunk, 8), :])
    for copy in stores:
        copy.wait()


def body(field, cotangent, w_approx, w_detail, w_point, bias):
    lat_tab, split_tab, join_tab = tables()
    wa = jnp.transpose(w_approx, (0, 2, 3, 1)).reshape(C, 16, C)
    wd = jnp.transpose(w_detail, (0, 1, 3, 4, 2)).reshape(3, C, 16, C)
    anywhere = pl.BlockSpec(memory_space=pl.ANY)
    vmem = pltpu.VMEM
    block = (32, 128)
    hbm = pl.BlockSpec(memory_space=pltpu.HBM)
    results = pl.pallas_call(
        kernel,
        out_shape=(
            vmem((PAIRS, 2 * C, W), F32),
            vmem((8,) + block, F32),
            vmem(block, F32),
            vmem((4, C, 16, C), F32),
            vmem((C, C), F32),
            vmem((1, C), F32),
            vmem((PAIRS * 16, 2 * C), F32),
            vmem((96, W), F32),
        ),
        in_specs=[hbm] * 9,
        out_specs=(pl.BlockSpec(memory_space=vmem),) * 8,
        scratch_shapes=[
            vmem((4, C, 8, W), F32),
            vmem((4, C, 8, W), F32),
            vmem((4, C, 16, C), F32),
            vmem((C, C), F32),
            vmem((1, C), F32),
            vmem((64, 2 * W), F32),
            vmem((C, C, 2 * C), BF16),
            vmem((3 * C, C), BF16),
            vmem((3 * C, C), BF16),
            vmem((PAIRS, 2 * C, W), F32),
            vmem((PAIRS * 2 * C, 2 * W), BF16),
            vmem((PAIRS * 2 * C, 2 * W), BF16),
            vmem((PAIRS, 32, 2 * C), F32),
            vmem((16, 32, 2 * C), F32),
            vmem((8,) + block, F32),
            vmem(block, F32),
            vmem((8,) + block, F32),
            vmem((8,) + block, F32),
            vmem((8,) + block, F32),
            vmem((8,) + block, F32),
            vmem(block, F32),
            vmem((8, 40, 128), F32),
            vmem((4, 40, 128), F32),
            vmem((4, 40, 128), F32),
            vmem((4, 40, 128), F32),
            pltpu.SemaphoreType.DMA((7,)),
            pltpu.SemaphoreType.DMA((8,)),
            pltpu.SemaphoreType.DMA((4, 7)),
            pltpu.SemaphoreType.DMA((4, 7)),
            pltpu.SemaphoreType.DMA((4, 7)),
            pltpu.SemaphoreType.DMA((4, 7)),
        ],
        compiler_params=pltpu.CompilerParams(
            collective_id=0, has_side_effects=True, vmem_limit_bytes=48 * 1024 * 1024
        ),
    )(
        *[
            pltpu.with_memory_space_constraint(x, pltpu.HBM)
            for x in (
                field,
                cotangent,
                wa,
                wd,
                w_point,
                bias.reshape(1, C),
                jnp.asarray(lat_tab),
                jnp.asarray(split_tab),
                jnp.asarray(join_tab),
            )
        ]
    )
    gfield, ga, gd, gp, gb = pl.pallas_call(
        last_kernel,
        out_shape=(
            jax.ShapeDtypeStruct((C, H, W), F32),
            jax.ShapeDtypeStruct((C, 16, C), F32),
            jax.ShapeDtypeStruct((3, C, 16, C), F32),
            jax.ShapeDtypeStruct((C, C), F32),
            jax.ShapeDtypeStruct((1, C), F32),
        ),
        in_specs=[pl.BlockSpec(memory_space=vmem)] * 8,
        out_specs=(anywhere,) * 5,
        scratch_shapes=[
            vmem((16, 32, 2 * C), F32),
            vmem((4, C, 8, W), F32),
            pltpu.SemaphoreType.DMA((10,)),
        ],
        compiler_params=pltpu.CompilerParams(vmem_limit_bytes=32 * 1024 * 1024),
    )(*[pltpu.with_memory_space_constraint(x, vmem) for x in results])
    ga = jnp.transpose(ga.reshape(C, 2, 8, C), (0, 3, 1, 2))
    gd = jnp.transpose(gd.reshape(3, C, 2, 8, C), (0, 1, 4, 2, 3))
    return gfield, ga, gd, gp, gb.reshape(C)


def solution(mesh):
    placed = (
        P(None, "lat", "lon"),
        P(None, "lat", "lon"),
        P(None, None, "lat", "lon"),
        P(None, None, None, "lat", "lon"),
        P(),
        P(),
    )
    return jax.shard_map(
        body,
        mesh=mesh,
        in_specs=placed,
        out_specs=(
            P(None, "lat", "lon"),
            P(None, None, "lat", "lon"),
            P(None, None, None, "lat", "lon"),
            P(),
            P(),
        ),
        check_vma=False,
    )
```

```python
import math

import numpy as np

import jax
import jax.numpy as jnp
from jax import lax
from jax.experimental import pallas as pl
from jax.experimental.pallas import tpu as pltpu
from jax.sharding import PartitionSpec as P

LOW = np.array(
    [
        0.23037781330885523,
        0.7148465705525415,
        0.6308807679295904,
        -0.02798376941698385,
        -0.18703481171888114,
        0.030841381835986965,
        0.032883011666982945,
        -0.010597401784997278,
    ],
    np.float64,
)
HIGH = np.array([LOW[7 - j] if j % 2 == 0 else -LOW[7 - j] for j in range(8)])

C = 64
H = 32
W = 128
LAT = 32
LON = 16
PAIRS = H // 2
F32 = jnp.float32
BF16 = jnp.bfloat16
MESH = pl.DeviceIdType.MESH


def long_filters():
    def spread(taps, step):
        out = np.zeros((len(taps) - 1) * step + 1)
        out[::step] = taps
        return out

    third = np.ones(1)
    for level in range(3):
        third = np.convolve(third, spread(LOW, 2**level))
    return [np.convolve(third, spread(LOW, 8)), np.convolve(third, spread(HIGH, 8))]


def tap(taps, at):
    return taps[at] if 0 <= at < len(taps) else 0.0


def tables():
    both = long_filters()
    lat = np.zeros((PAIRS, 4, 2, 2, 2, C))
    for h2 in range(PAIRS):
        for dl in range(4):
            for u in range(2):
                for ii in range(2):
                    for p in range(2):
                        lat[h2, dl, u, ii, p, :] = tap(both[u], 2 * h2 + p + 32 * dl - 16 * ii)
    lat = lat.reshape(PAIRS * 16, 2 * C).astype(np.float32)
    lon = np.zeros((2, 2, 8, W))
    for ds in range(2):
        for v in range(2):
            for jj in range(8):
                for w in range(W):
                    lon[ds, v, jj, w] = tap(both[v], w + 128 * ds - 16 * jj)
    lon = lon.reshape(32, W).astype(np.float32)
    high = lon.astype(jnp.bfloat16).astype(np.float32)
    rest = (lon - high).astype(jnp.bfloat16).astype(np.float32)
    split = np.concatenate(
        [np.concatenate([high, high], 1), np.concatenate([rest, np.zeros_like(rest)], 1)], 0
    )
    join = np.concatenate([high, rest, high], 0)
    return lat, split, join


USED = (tables()[0].reshape(PAIRS, 4, 4, 2 * C) != 0).any(axis=3).tolist()


def halves(x):
    high = x.astype(BF16)
    return high, (x - high.astype(F32)).astype(BF16)


def swap(x):
    return pltpu.roll(x, 64, axis=1)


def dot_nt(a, b):
    return lax.dot_general(a, b, (((1,), (1,)), ((), ())), preferred_element_type=F32)


def dot_tn(a, b):
    return lax.dot_general(a, b, (((0,), (0,)), ((), ())), preferred_element_type=F32)


def gelu_slope(p):
    cdf = 0.5 * (1.0 + lax.erf(p * (1.0 / math.sqrt(2.0))))
    pdf = jnp.exp(-0.5 * p * p) * (1.0 / math.sqrt(2.0 * math.pi))
    return cdf + p * pdf


def lat_join(recv, own, dup, left):
    for dl in range(4):
        blocks = [own[...] if (dl, ds) == (0, 0) else recv[dl * 2 + ds] for ds in range(2)]
        for u in range(2):
            rows = jnp.concatenate([b[u * 16:(u + 1) * 16] for b in blocks], 0)
            turned = swap(rows)
            dup[dl * 4 + u * 2] = jnp.where(left, rows, turned)
            dup[dl * 4 + u * 2 + 1] = jnp.where(left, turned, rows)


def lon_join(h2, dup, lat_tab, join_tab):
    total = jnp.zeros((32, 2 * C), F32)
    for m in range(16):
        total = total + lat_tab[pl.ds(h2 * 16 + m, 1), :] * dup[m]
    high, rest = halves(total)
    return dot_tn(jnp.concatenate([high, high, rest], 0), join_tab[...].astype(BF16))


def kernel(
    field, cot, wa, wd, wpoint, bias, lat_hbm, split_hbm, join_hbm,
    base, recv4, send4, out_gw, out_gp, out_gb, lat_tab, join_tab,
    fbuf, cbuf, wbuf, wpbuf, biasbuf, split_tab,
    wmix, wfwd, wbwd, grad, thl, ghl, yscr, dup,
    send1, send2, send3, recv1, recv2, recv3, coarse,
    red1, red2, red3, red4,
    load_sem, fload_sem, send_sem, recv_sem, rsend_sem, rrecv_sem,
):
    lat_at = lax.axis_index("lat")
    lon_at = lax.axis_index("lon")
    left = lax.broadcasted_iota(jnp.int32, (32, 2 * C), 1) < C

    steps = [(2, 1), (1, 1), (3, 1), (0, 1), (2, 0), (1, 0), (3, 0)]
    behind = [(lax.rem(lat_at + (LAT - dl), LAT), lax.rem(lon_at + (LON - ds), LON)) for dl, ds in steps]
    ahead = [(lax.rem(lat_at + dl, LAT), lax.rem(lon_at + ds, LON)) for dl, ds in steps]
    zhi = lon_at // 8
    x_at = lax.rem(lon_at, 8) // 2
    core = lax.rem(lon_at, 2)
    y_at = lax.rem(lat_at, 4)
    zlo = lat_at // 4
    run, inner = zhi * 2 + zlo // 4, lax.rem(zlo, 4)

    def at(z_run, z_inner):
        return (lax.rem(z_run, 2) * 16 + z_inner * 4 + y_at, (z_run // 2) * 8 + lax.rem(lon_at, 8))

    turns = [lambda i, d=d: lax.rem(i + d, 4) for d in (2, 1, 3)]
    same_core = [(zlo * 4 + t(y_at), lon_at) for t in turns]
    other_core = [(zlo * 4 + t(y_at), lon_at + 1 - 2 * core) for t in turns]
    sum_steps = [
        (run, [at(t(run), inner) for t in turns]),
        (inner, [at(run, t(inner)) for t in turns]),
        (x_at, [(lat_at, zhi * 8 + t(x_at) * 2 + core) for t in turns]),
        (core * 4 + y_at, same_core + other_core + [(lat_at, lon_at + 1 - 2 * core)]),
    ]

    barrier = pltpu.get_barrier_semaphore()
    everyone = ahead + behind + sum_steps[0][1] + sum_steps[1][1] + sum_steps[2][1] + other_core

    for device in everyone:
        pl.semaphore_signal(barrier, inc=1, device_id=device, device_id_type=MESH)

    field_loads = [
        pltpu.make_async_copy(field.at[:, pl.ds(8 * q, 8), :], fbuf.at[q], fload_sem.at[q]) for q in range(4)
    ]
    for load in field_loads:
        load.start()
    split_load = pltpu.make_async_copy(split_hbm, split_tab, load_sem.at[0])
    lat_load = pltpu.make_async_copy(lat_hbm, lat_tab, load_sem.at[1])
    wp_load = pltpu.make_async_copy(wpoint, wpbuf, load_sem.at[2])
    bias_load = pltpu.make_async_copy(bias, biasbuf, load_sem.at[3])
    wa_load = pltpu.make_async_copy(wa, wbuf.at[0], load_sem.at[4])
    wd_load = pltpu.make_async_copy(wd, wbuf.at[pl.ds(1, 3)], load_sem.at[5])
    cot_loads = [
        pltpu.make_async_copy(cot.at[:, pl.ds(8 * q, 8), :], cbuf.at[q], fload_sem.at[4 + q]) for q in range(4)
    ]
    join_load = pltpu.make_async_copy(join_hbm, join_tab, load_sem.at[6])
    for load in [split_load, lat_load, wp_load, bias_load, wa_load, wd_load, join_load] + cot_loads:
        load.start()

    def cell_pair(buffer, h2):
        chunk, row = h2 // 4, (h2 % 4) * 2
        flat = buffer.at[chunk].reshape(C * 8, W)
        return jnp.concatenate([flat[pl.ds(row + p, C, stride=8), :] for p in range(2)], 0)

    def lon_split(rows, at):
        both = dot_nt(split_tab[...].astype(BF16), rows)
        sums = both[:32] + both[32:]
        yscr[at, :, :] = sums[:, :128]
        yscr[at + 1, :, :] = sums[:, 128:]

    def lat_split(buffer, send):
        for dl in (2, 1, 3, 0):
            sums = [None] * 4
            for h2 in range(PAIRS):
                y = yscr[h2]
                for m in range(4):
                    if USED[h2][dl][m]:
                        term = lat_tab[pl.ds(h2 * 16 + dl * 4 + m, 1), :] * y
                        sums[m] = term if sums[m] is None else sums[m] + term
            for u in range(2):
                first, second = sums[2 * u], sums[2 * u + 1]
                modes = jnp.where(left, first, second) + swap(jnp.where(left, second, first))
                for ds in range(2):
                    buffer[dl * 2 + ds, u * 16:(u + 1) * 16, :] = modes[ds * 16:(ds + 1) * 16]
            send(dl, 1)
        for dl in (2, 1, 3):
            send(dl, 0)

    def exchange(number, source_of, recv, targets):
        return [
            pltpu.make_async_remote_copy(
                src_ref=source_of(dl * 2 + ds),
                dst_ref=recv.at[dl * 2 + ds],
                send_sem=send_sem.at[number, n],
                recv_sem=recv_sem.at[number, n],
                device_id=targets[n],
                device_id_type=MESH,
            )
            for n, (dl, ds) in enumerate(steps)
        ]

    def point_map(weights, rows):
        high = [rows[64 * n:64 * n + 64, :W] for n in range(4)]
        rest = [rows[64 * n:64 * n + 64, W:] for n in range(4)]
        high = jnp.concatenate(high, 1)
        rest = jnp.concatenate(rest, 1)
        out = dot_tn(weights, jnp.concatenate([high, rest, high], 0))
        return jnp.concatenate([out[:, W * n:W * n + W] for n in range(4)], 0)

    split_load.wait()
    for q in range(4):
        field_loads[q].wait()
        for n in range(2):
            h2 = q * 4 + n * 2
            for k in range(2):
                high, rest = halves(cell_pair(fbuf, h2 + k))
                thl[(h2 + k) * 128:(h2 + k + 1) * 128, :W] = high
                thl[(h2 + k) * 128:(h2 + k + 1) * 128, W:] = rest
            lon_split(thl[h2 * 128:h2 * 128 + 256, :], h2)
    lat_load.wait()
    lat_split(send1, lambda dl, ds: None)
    pl.semaphore_wait(barrier, len(everyone))
    copies1 = exchange(0, lambda n: send1.at[n], recv1, behind)
    for copy in copies1:
        copy.start()

    wp_load.wait()
    bias_load.wait()
    high, rest = halves(wpbuf[...])
    wbwd[...] = jnp.concatenate([high, high, rest], 0)
    high, rest = halves(wpbuf[...].T)
    wfwd[...] = jnp.concatenate([high, high, rest], 0)
    bias_cells = jnp.broadcast_to(biasbuf[...], (W, C)).T
    bias_cells = jnp.concatenate([bias_cells, bias_cells], 0)
    for h4 in range(PAIRS // 2):
        mapped = point_map(wfwd[...], thl[h4 * 256:h4 * 256 + 256, :])
        for k in range(2):
            h2 = 2 * h4 + k
            base[h2] = mapped[128 * k:128 * k + 128] + cell_pair(fbuf, h2) + bias_cells
    wa_load.wait()
    wd_load.wait()

    def prepare(b, carry):
        flat = wbuf.at[b].reshape(C * 16, C)
        for n in range(16):
            one = flat[pl.ds(n, C, stride=16), :]
            high = one.astype(BF16).astype(F32)
            wmix[b * 16 + n] = jnp.concatenate([high, one - high], 1).astype(BF16)
        return carry

    lax.fori_loop(0, 4, prepare, 0)

    total = send1[0]
    for n, (dl, ds) in enumerate(steps):
        copies1[n].wait_recv()
        total = total + recv1[dl * 2 + ds]
    coarse[...] = total

    row8 = lax.broadcasted_iota(jnp.int32, (8, 2 * C), 0)
    half8 = lax.broadcasted_iota(jnp.int32, (8, 2 * C), 1) // C
    left8 = half8 == 0

    def stacked(x):
        high = x.astype(BF16).astype(F32)
        return jnp.concatenate([high, x - high], 0).astype(BF16)

    mixed = []
    for b in range(4):
        both = []
        for ii in range(2):
            rows = total[8 * b:8 * b + 8]
            lhs = stacked((rows if ii == 0 else swap(rows))[:, :C])
            kept = jnp.zeros((8, 2 * C), F32)
            for j2 in range(4):
                at = b * 16 + ii * 8 + j2 * 2
                out = jnp.dot(lhs, jnp.concatenate([wmix[at], wmix[at + 1]], 1), preferred_element_type=F32)
                out = out[:8] + out[8:]
                kept = jnp.where(row8 == 2 * j2, out[:, :128], kept)
                kept = jnp.where(row8 == 2 * j2 + 1, out[:, 128:], kept)
            both.append(kept + swap(kept))
        mixed.append(jnp.where(left8, both[0], both[1]))
    send2[...] = jnp.concatenate(mixed, 0) - total
    copies2 = exchange(1, lambda n: send2, recv2, ahead)
    for copy in copies2:
        copy.start()

    join_load.wait()
    for load in cot_loads:
        load.wait()
    for copy in copies2:
        copy.wait_recv()
    lat_join(recv2, send2, dup, left)

    for h2 in range(PAIRS):
        base[h2] = base[h2] + lon_join(h2, dup, lat_tab, join_tab)
    for h2 in range(PAIRS):
        g = gelu_slope(base[h2]) * cell_pair(cbuf, h2)
        grad[h2] = g
        high, rest = halves(g)
        ghl[h2 * 128:(h2 + 1) * 128, :W] = high
        ghl[h2 * 128:(h2 + 1) * 128, W:] = rest
    for h4 in range(PAIRS // 2):
        lon_split(ghl[h4 * 256:h4 * 256 + 256, :], 2 * h4)
    copies3 = exchange(2, lambda n: send3.at[n], recv3, behind)
    lat_split(send3, lambda dl, ds: copies3[steps.index((dl, ds))].start())

    point = jnp.zeros((128, 128), F32)
    rows_sum = jnp.zeros((C, W), F32)
    for h2 in range(PAIRS):
        at = h2 * 128
        both = []
        for source in (ghl, thl):
            tops = jnp.concatenate([source[at:at + 64, :W], source[at + 64:at + 128, :W]], 1)
            rests = jnp.concatenate([source[at:at + 64, W:], source[at + 64:at + 128, W:]], 1)
            both.append(jnp.concatenate([tops, rests], 0))
        point = point + dot_nt(both[0], both[1])
        rows_sum = rows_sum + grad[h2, 0:64, :] + grad[h2, 64:128, :]
    point = point[:C] + point[C:]
    point = point + swap(point)
    bias_term = jnp.sum(rows_sum, axis=1, keepdims=True)
    sums_of = [red1, red2, red3, red4]
    folded = jnp.concatenate([point[: C // 2, :C], point[C // 2:, :C]], 1)
    bias_row = jnp.broadcast_to(bias_term, (C, 128)).T[:8]
    first = jnp.concatenate([folded, jnp.concatenate([bias_row, bias_row], 1)], 0)
    reduces = []

    def send_sum(number, rows):
        own, ids = sum_steps[number]
        ref = sums_of[number]
        ref[pl.ds(own, 1)] = rows[None]
        copies = [
            pltpu.make_async_remote_copy(
                src_ref=ref.at[own],
                dst_ref=ref.at[own],
                send_sem=rsend_sem.at[number, n],
                recv_sem=rrecv_sem.at[number, n],
                device_id=device,
                device_id_type=MESH,
            )
            for n, device in enumerate(ids)
        ]
        for copy in copies:
            copy.start()
        reduces.append(copies)

    def take_sum(number):
        for copy in reduces[number]:
            copy.wait_recv()
        ref = sums_of[number]
        rows = ref[0]
        for n in range(1, len(reduces[number]) + 1):
            rows = rows + ref[n]
        return rows

    send_sum(0, first)

    for h4 in range(PAIRS // 2):
        mapped = point_map(wbwd[...], ghl[h4 * 256:h4 * 256 + 256, :])
        for k in range(2):
            h2 = 2 * h4 + k
            base[h2] = mapped[128 * k:128 * k + 128] + grad[h2]

    gtotal = send3[0]
    for n, (dl, ds) in enumerate(steps):
        copies3[n].wait_recv()
        gtotal = gtotal + recv3[dl * 2 + ds]

    def unpacked(rows, b):
        part = rows[8 * b:8 * b + 8]
        return jnp.concatenate([part[:, :C], part[:, C:]], 0)

    gmodes = [unpacked(gtotal, b) for b in range(4)]
    backs = []
    for b in range(4):
        rows = gtotal[8 * b:8 * b + 8]
        turned = swap(rows)
        both = []
        for ii in range(2):
            lhs = stacked(jnp.where(left8, rows, turned) if ii == 0 else jnp.where(left8, turned, rows))
            maps = wmix[b * 16 + ii * 8:b * 16 + ii * 8 + 8].reshape(8 * C, 2 * C)
            out = dot_nt(lhs, maps)
            out = out[:8] + out[8:]
            kept = jnp.zeros((8, 2 * C), F32)
            for j2 in range(4):
                part = out[:, 128 * j2:128 * j2 + 128]
                kept = jnp.where(row8 - half8 == 2 * j2, part, kept)
            both.append(kept + swap(kept))
        backs.append(jnp.where(left8, both[0], both[1]))
    send4[...] = jnp.concatenate(backs, 0) - gtotal
    copies4 = exchange(3, lambda n: send4, recv4, ahead)
    for copy in copies4:
        copy.start()

    send_sum(1, take_sum(0))

    def outer(g, turned):
        for k in range(8):
            for b in range(4):
                rows = turned[8 * b:8 * b + 8]
                column = jnp.concatenate([rows[:, k:k + 1], rows[:, C + k:C + k + 1]], 0)
                out_gw[b, g * 8 + k] = column * gmodes[b]
        return pltpu.roll(turned, 2 * C - 8, axis=1)

    lax.fori_loop(0, C // 8, outer, coarse[...])
    send_sum(2, take_sum(1))
    send_sum(3, take_sum(2))
    for copy in copies4:
        copy.wait_recv()
    rows = take_sum(3)
    out_gp[...] = jnp.concatenate([rows[: C // 2, :C], rows[: C // 2, C:]], 0)
    out_gb[...] = rows[C // 2:C // 2 + 1, :C]
    for copy in copies1 + copies2 + copies3 + copies4 + sum(reduces, []):
        copy.wait_send()


def last_kernel(
    base, recv4, send4, gw, gp, gb, lat_tab, join_tab, out_field, out_ga, out_gd, out_gp, out_gb, dup, obuf, sem
):
    stores = []

    def store(src, dst):
        stores.append(pltpu.make_async_copy(src, dst, sem.at[len(stores)]))
        stores[-1].start()

    store(gw.at[0], out_ga)
    for b in range(3):
        store(gw.at[1 + b], out_gd.at[b])
    store(gp, out_gp)
    store(gb, out_gb)
    left = lax.broadcasted_iota(jnp.int32, (32, 2 * C), 1) < C
    lat_join(recv4, send4, dup, left)
    for h2 in range(PAIRS):
        cells = base[h2] + lon_join(h2, dup, lat_tab, join_tab)
        chunk, row = h2 // 4, (h2 % 4) * 2
        flat = obuf.at[chunk].reshape(C * 8, W)
        for p in range(2):
            flat[pl.ds(row + p, C, stride=8), :] = cells[64 * p:64 * p + 64]
        if h2 % 4 == 3:
            store(obuf.at[chunk], out_field.at[:, pl.ds(8 * chunk, 8), :])
    for copy in stores:
        copy.wait()


def body(field, cotangent, w_approx, w_detail, w_point, bias):
    lat_tab, split_tab, join_tab = tables()
    wa = jnp.transpose(w_approx, (0, 2, 3, 1)).reshape(C, 16, C)
    wd = jnp.transpose(w_detail, (0, 1, 3, 4, 2)).reshape(3, C, 16, C)
    anywhere = pl.BlockSpec(memory_space=pl.ANY)
    vmem = pltpu.VMEM
    block = (32, 128)
    hbm = pl.BlockSpec(memory_space=pltpu.HBM)
    results = pl.pallas_call(
        kernel,
        out_shape=(
            vmem((PAIRS, 2 * C, W), F32),
            vmem((8,) + block, F32),
            vmem(block, F32),
            vmem((4, C, 16, C), F32),
            vmem((C, C), F32),
            vmem((1, C), F32),
            vmem((PAIRS * 16, 2 * C), F32),
            vmem((96, W), F32),
        ),
        in_specs=[hbm] * 9,
        out_specs=(pl.BlockSpec(memory_space=vmem),) * 8,
        scratch_shapes=[
            vmem((4, C, 8, W), F32),
            vmem((4, C, 8, W), F32),
            vmem((4, C, 16, C), F32),
            vmem((C, C), F32),
            vmem((1, C), F32),
            vmem((64, 2 * W), F32),
            vmem((C, C, 2 * C), BF16),
            vmem((3 * C, C), BF16),
            vmem((3 * C, C), BF16),
            vmem((PAIRS, 2 * C, W), F32),
            vmem((PAIRS * 2 * C, 2 * W), BF16),
            vmem((PAIRS * 2 * C, 2 * W), BF16),
            vmem((PAIRS, 32, 2 * C), F32),
            vmem((16, 32, 2 * C), F32),
            vmem((8,) + block, F32),
            vmem(block, F32),
            vmem((8,) + block, F32),
            vmem((8,) + block, F32),
            vmem((8,) + block, F32),
            vmem((8,) + block, F32),
            vmem(block, F32),
            vmem((4, 40, 128), F32),
            vmem((4, 40, 128), F32),
            vmem((4, 40, 128), F32),
            vmem((8, 40, 128), F32),
            pltpu.SemaphoreType.DMA((7,)),
            pltpu.SemaphoreType.DMA((8,)),
            pltpu.SemaphoreType.DMA((4, 7)),
            pltpu.SemaphoreType.DMA((4, 7)),
            pltpu.SemaphoreType.DMA((4, 7)),
            pltpu.SemaphoreType.DMA((4, 7)),
        ],
        compiler_params=pltpu.CompilerParams(
            collective_id=0, has_side_effects=True, vmem_limit_bytes=48 * 1024 * 1024
        ),
    )(
        *[
            pltpu.with_memory_space_constraint(x, pltpu.HBM)
            for x in (
                field,
                cotangent,
                wa,
                wd,
                w_point,
                bias.reshape(1, C),
                jnp.asarray(lat_tab),
                jnp.asarray(split_tab),
                jnp.asarray(join_tab),
            )
        ]
    )
    gfield, ga, gd, gp, gb = pl.pallas_call(
        last_kernel,
        out_shape=(
            jax.ShapeDtypeStruct((C, H, W), F32),
            jax.ShapeDtypeStruct((C, 16, C), F32),
            jax.ShapeDtypeStruct((3, C, 16, C), F32),
            jax.ShapeDtypeStruct((C, C), F32),
            jax.ShapeDtypeStruct((1, C), F32),
        ),
        in_specs=[pl.BlockSpec(memory_space=vmem)] * 8,
        out_specs=(anywhere,) * 5,
        scratch_shapes=[
            vmem((16, 32, 2 * C), F32),
            vmem((4, C, 8, W), F32),
            pltpu.SemaphoreType.DMA((10,)),
        ],
        compiler_params=pltpu.CompilerParams(vmem_limit_bytes=32 * 1024 * 1024),
    )(*[pltpu.with_memory_space_constraint(x, vmem) for x in results])
    ga = jnp.transpose(ga.reshape(C, 2, 8, C), (0, 3, 1, 2))
    gd = jnp.transpose(gd.reshape(3, C, 2, 8, C), (0, 1, 4, 2, 3))
    return gfield, ga, gd, gp, gb.reshape(C)


def solution(mesh):
    placed = (
        P(None, "lat", "lon"),
        P(None, "lat", "lon"),
        P(None, None, "lat", "lon"),
        P(None, None, None, "lat", "lon"),
        P(),
        P(),
    )
    return jax.shard_map(
        body,
        mesh=mesh,
        in_specs=placed,
        out_specs=(
            P(None, "lat", "lon"),
            P(None, None, "lat", "lon"),
            P(None, None, None, "lat", "lon"),
            P(),
            P(),
        ),
        check_vma=False,
    )
```

```python
import math

import numpy as np

import jax
import jax.numpy as jnp
from jax import lax
from jax.experimental import pallas as pl
from jax.experimental.pallas import tpu as pltpu
from jax.sharding import PartitionSpec as P

LOW = np.array(
    [
        0.23037781330885523,
        0.7148465705525415,
        0.6308807679295904,
        -0.02798376941698385,
        -0.18703481171888114,
        0.030841381835986965,
        0.032883011666982945,
        -0.010597401784997278,
    ],
    np.float64,
)
HIGH = np.array([LOW[7 - j] if j % 2 == 0 else -LOW[7 - j] for j in range(8)])

C = 64
H = 32
W = 128
LAT = 32
LON = 16
PAIRS = H // 2
F32 = jnp.float32
BF16 = jnp.bfloat16
MESH = pl.DeviceIdType.MESH


def long_filters():
    def spread(taps, step):
        out = np.zeros((len(taps) - 1) * step + 1)
        out[::step] = taps
        return out

    third = np.ones(1)
    for level in range(3):
        third = np.convolve(third, spread(LOW, 2**level))
    return [np.convolve(third, spread(LOW, 8)), np.convolve(third, spread(HIGH, 8))]


def tap(taps, at):
    return taps[at] if 0 <= at < len(taps) else 0.0


def tables():
    both = long_filters()
    lat = np.zeros((PAIRS, 4, 2, 2, 2, C))
    for h2 in range(PAIRS):
        for dl in range(4):
            for u in range(2):
                for ii in range(2):
                    for p in range(2):
                        lat[h2, dl, u, ii, p, :] = tap(both[u], 2 * h2 + p + 32 * dl - 16 * ii)
    lat = lat.reshape(PAIRS * 16, 2 * C).astype(np.float32)
    lon = np.zeros((2, 2, 8, W))
    for ds in range(2):
        for v in range(2):
            for jj in range(8):
                for w in range(W):
                    lon[ds, v, jj, w] = tap(both[v], w + 128 * ds - 16 * jj)
    lon = lon.reshape(32, W).astype(np.float32)
    high = lon.astype(jnp.bfloat16).astype(np.float32)
    rest = (lon - high).astype(jnp.bfloat16).astype(np.float32)
    split = np.concatenate(
        [np.concatenate([high, high], 1), np.concatenate([rest, np.zeros_like(rest)], 1)], 0
    )
    join = np.concatenate([high, rest, high], 0)
    return lat, split, join


USED = (tables()[0].reshape(PAIRS, 4, 4, 2 * C) != 0).any(axis=3).tolist()


def halves(x):
    high = x.astype(BF16)
    return high, (x - high.astype(F32)).astype(BF16)


def swap(x):
    return pltpu.roll(x, 64, axis=1)


def dot_nt(a, b):
    return lax.dot_general(a, b, (((1,), (1,)), ((), ())), preferred_element_type=F32)


def dot_tn(a, b):
    return lax.dot_general(a, b, (((0,), (0,)), ((), ())), preferred_element_type=F32)


def gelu_slope(p):
    cdf = 0.5 * (1.0 + lax.erf(p * (1.0 / math.sqrt(2.0))))
    pdf = jnp.exp(-0.5 * p * p) * (1.0 / math.sqrt(2.0 * math.pi))
    return cdf + p * pdf


def lat_join(recv, own, dup, left):
    for dl in range(4):
        blocks = [own[...] if (dl, ds) == (0, 0) else recv[dl * 2 + ds] for ds in range(2)]
        for u in range(2):
            rows = jnp.concatenate([b[u * 16:(u + 1) * 16] for b in blocks], 0)
            turned = swap(rows)
            dup[dl * 4 + u * 2] = jnp.where(left, rows, turned)
            dup[dl * 4 + u * 2 + 1] = jnp.where(left, turned, rows)


def lon_join(h2, dup, lat_tab, join_tab):
    total = jnp.zeros((32, 2 * C), F32)
    for m in range(16):
        total = total + lat_tab[pl.ds(h2 * 16 + m, 1), :] * dup[m]
    high, rest = halves(total)
    return dot_tn(jnp.concatenate([high, high, rest], 0), join_tab[...].astype(BF16))


def kernel(
    field, cot, wa, wd, wpoint, bias, lat_hbm, split_hbm, join_hbm,
    base, recv4, send4, out_gw, out_gp, out_gb, lat_tab, join_tab,
    fbuf, cbuf, wbuf, wpbuf, biasbuf, split_tab,
    wmix, wfwd, wbwd, grad, thl, ghl, yscr, dup,
    send1, send2, send3, recv1, recv2, recv3, coarse,
    red1, red2, red3, red4,
    load_sem, fload_sem, send_sem, recv_sem, rsend_sem, rrecv_sem,
):
    lat_at = lax.axis_index("lat")
    lon_at = lax.axis_index("lon")
    left = lax.broadcasted_iota(jnp.int32, (32, 2 * C), 1) < C

    steps = [(2, 1), (1, 1), (3, 1), (0, 1), (2, 0), (1, 0), (3, 0)]
    behind = [(lax.rem(lat_at + (LAT - dl), LAT), lax.rem(lon_at + (LON - ds), LON)) for dl, ds in steps]
    ahead = [(lax.rem(lat_at + dl, LAT), lax.rem(lon_at + ds, LON)) for dl, ds in steps]
    zhi = lon_at // 8
    x_at = lax.rem(lon_at, 8) // 2
    core = lax.rem(lon_at, 2)
    y_at = lax.rem(lat_at, 4)
    zlo = lat_at // 4
    run, inner = zhi * 2 + zlo // 4, lax.rem(zlo, 4)

    def at(z_run, z_inner):
        return (lax.rem(z_run, 2) * 16 + z_inner * 4 + y_at, (z_run // 2) * 8 + lax.rem(lon_at, 8))

    turns = [lambda i, d=d: lax.rem(i + d, 4) for d in (2, 1, 3)]
    same_core = [(zlo * 4 + t(y_at), lon_at) for t in turns]
    other_core = [(zlo * 4 + t(y_at), lon_at + 1 - 2 * core) for t in turns]
    sum_steps = [
        (core * 4 + y_at, same_core + other_core + [(lat_at, lon_at + 1 - 2 * core)]),
        (x_at, [(lat_at, zhi * 8 + t(x_at) * 2 + core) for t in turns]),
        (inner, [at(run, t(inner)) for t in turns]),
        (run, [at(t(run), inner) for t in turns]),
    ]

    barrier = pltpu.get_barrier_semaphore()
    everyone = ahead + behind + sum_steps[3][1] + sum_steps[2][1] + sum_steps[1][1] + other_core

    for device in everyone:
        pl.semaphore_signal(barrier, inc=1, device_id=device, device_id_type=MESH)

    field_loads = [
        pltpu.make_async_copy(field.at[:, pl.ds(8 * q, 8), :], fbuf.at[q], fload_sem.at[q]) for q in range(4)
    ]
    for load in field_loads:
        load.start()
    split_load = pltpu.make_async_copy(split_hbm, split_tab, load_sem.at[0])
    lat_load = pltpu.make_async_copy(lat_hbm, lat_tab, load_sem.at[1])
    wp_load = pltpu.make_async_copy(wpoint, wpbuf, load_sem.at[2])
    bias_load = pltpu.make_async_copy(bias, biasbuf, load_sem.at[3])
    wa_load = pltpu.make_async_copy(wa, wbuf.at[0], load_sem.at[4])
    wd_load = pltpu.make_async_copy(wd, wbuf.at[pl.ds(1, 3)], load_sem.at[5])
    cot_loads = [
        pltpu.make_async_copy(cot.at[:, pl.ds(8 * q, 8), :], cbuf.at[q], fload_sem.at[4 + q]) for q in range(4)
    ]
    join_load = pltpu.make_async_copy(join_hbm, join_tab, load_sem.at[6])
    for load in [split_load, lat_load, wp_load, bias_load, wa_load, wd_load, join_load] + cot_loads:
        load.start()

    def cell_pair(buffer, h2):
        chunk, row = h2 // 4, (h2 % 4) * 2
        flat = buffer.at[chunk].reshape(C * 8, W)
        return jnp.concatenate([flat[pl.ds(row + p, C, stride=8), :] for p in range(2)], 0)

    def lon_split(rows, at):
        both = dot_nt(split_tab[...].astype(BF16), rows)
        sums = both[:32] + both[32:]
        yscr[at, :, :] = sums[:, :128]
        yscr[at + 1, :, :] = sums[:, 128:]

    def lat_split(buffer, send):
        for dl in (2, 1, 3, 0):
            sums = [None] * 4
            for h2 in range(PAIRS):
                y = yscr[h2]
                for m in range(4):
                    if USED[h2][dl][m]:
                        term = lat_tab[pl.ds(h2 * 16 + dl * 4 + m, 1), :] * y
                        sums[m] = term if sums[m] is None else sums[m] + term
            for u in range(2):
                first, second = sums[2 * u], sums[2 * u + 1]
                modes = jnp.where(left, first, second) + swap(jnp.where(left, second, first))
                for ds in range(2):
                    buffer[dl * 2 + ds, u * 16:(u + 1) * 16, :] = modes[ds * 16:(ds + 1) * 16]
            send(dl, 1)
        for dl in (2, 1, 3):
            send(dl, 0)

    def exchange(number, source_of, recv, targets):
        return [
            pltpu.make_async_remote_copy(
                src_ref=source_of(dl * 2 + ds),
                dst_ref=recv.at[dl * 2 + ds],
                send_sem=send_sem.at[number, n],
                recv_sem=recv_sem.at[number, n],
                device_id=targets[n],
                device_id_type=MESH,
            )
            for n, (dl, ds) in enumerate(steps)
        ]

    def point_map(weights, rows):
        high = [rows[64 * n:64 * n + 64, :W] for n in range(4)]
        rest = [rows[64 * n:64 * n + 64, W:] for n in range(4)]
        high = jnp.concatenate(high, 1)
        rest = jnp.concatenate(rest, 1)
        out = dot_tn(weights, jnp.concatenate([high, rest, high], 0))
        return jnp.concatenate([out[:, W * n:W * n + W] for n in range(4)], 0)

    split_load.wait()
    for q in range(4):
        field_loads[q].wait()
        for n in range(2):
            h2 = q * 4 + n * 2
            for k in range(2):
                high, rest = halves(cell_pair(fbuf, h2 + k))
                thl[(h2 + k) * 128:(h2 + k + 1) * 128, :W] = high
                thl[(h2 + k) * 128:(h2 + k + 1) * 128, W:] = rest
            lon_split(thl[h2 * 128:h2 * 128 + 256, :], h2)
    lat_load.wait()
    lat_split(send1, lambda dl, ds: None)
    pl.semaphore_wait(barrier, len(everyone))
    copies1 = exchange(0, lambda n: send1.at[n], recv1, behind)
    for copy in copies1:
        copy.start()

    wp_load.wait()
    bias_load.wait()
    high, rest = halves(wpbuf[...])
    wbwd[...] = jnp.concatenate([high, high, rest], 0)
    high, rest = halves(wpbuf[...].T)
    wfwd[...] = jnp.concatenate([high, high, rest], 0)
    bias_cells = jnp.broadcast_to(biasbuf[...], (W, C)).T
    bias_cells = jnp.concatenate([bias_cells, bias_cells], 0)
    for h4 in range(PAIRS // 2):
        mapped = point_map(wfwd[...], thl[h4 * 256:h4 * 256 + 256, :])
        for k in range(2):
            h2 = 2 * h4 + k
            base[h2] = mapped[128 * k:128 * k + 128] + cell_pair(fbuf, h2) + bias_cells
    wa_load.wait()
    wd_load.wait()

    def prepare(b, carry):
        flat = wbuf.at[b].reshape(C * 16, C)
        for n in range(16):
            one = flat[pl.ds(n, C, stride=16), :]
            high = one.astype(BF16).astype(F32)
            wmix[b * 16 + n] = jnp.concatenate([high, one - high], 1).astype(BF16)
        return carry

    lax.fori_loop(0, 4, prepare, 0)

    total = send1[0]
    for n, (dl, ds) in enumerate(steps):
        copies1[n].wait_recv()
        total = total + recv1[dl * 2 + ds]
    coarse[...] = total

    row8 = lax.broadcasted_iota(jnp.int32, (8, 2 * C), 0)
    half8 = lax.broadcasted_iota(jnp.int32, (8, 2 * C), 1) // C
    left8 = half8 == 0

    def stacked(x):
        high = x.astype(BF16).astype(F32)
        return jnp.concatenate([high, x - high], 0).astype(BF16)

    mixed = []
    for b in range(4):
        both = []
        for ii in range(2):
            rows = total[8 * b:8 * b + 8]
            lhs = stacked((rows if ii == 0 else swap(rows))[:, :C])
            kept = jnp.zeros((8, 2 * C), F32)
            for j2 in range(4):
                at = b * 16 + ii * 8 + j2 * 2
                out = jnp.dot(lhs, jnp.concatenate([wmix[at], wmix[at + 1]], 1), preferred_element_type=F32)
                out = out[:8] + out[8:]
                kept = jnp.where(row8 == 2 * j2, out[:, :128], kept)
                kept = jnp.where(row8 == 2 * j2 + 1, out[:, 128:], kept)
            both.append(kept + swap(kept))
        mixed.append(jnp.where(left8, both[0], both[1]))
    send2[...] = jnp.concatenate(mixed, 0) - total
    copies2 = exchange(1, lambda n: send2, recv2, ahead)
    for copy in copies2:
        copy.start()

    join_load.wait()
    for load in cot_loads:
        load.wait()
    for copy in copies2:
        copy.wait_recv()
    lat_join(recv2, send2, dup, left)

    for h2 in range(PAIRS):
        base[h2] = base[h2] + lon_join(h2, dup, lat_tab, join_tab)
    for h2 in range(PAIRS):
        g = gelu_slope(base[h2]) * cell_pair(cbuf, h2)
        grad[h2] = g
        high, rest = halves(g)
        ghl[h2 * 128:(h2 + 1) * 128, :W] = high
        ghl[h2 * 128:(h2 + 1) * 128, W:] = rest
    for h4 in range(PAIRS // 2):
        lon_split(ghl[h4 * 256:h4 * 256 + 256, :], 2 * h4)
    copies3 = exchange(2, lambda n: send3.at[n], recv3, behind)
    lat_split(send3, lambda dl, ds: copies3[steps.index((dl, ds))].start())

    point = jnp.zeros((128, 128), F32)
    rows_sum = jnp.zeros((C, W), F32)
    for h2 in range(PAIRS):
        at = h2 * 128
        both = []
        for source in (ghl, thl):
            tops = jnp.concatenate([source[at:at + 64, :W], source[at + 64:at + 128, :W]], 1)
            rests = jnp.concatenate([source[at:at + 64, W:], source[at + 64:at + 128, W:]], 1)
            both.append(jnp.concatenate([tops, rests], 0))
        point = point + dot_nt(both[0], both[1])
        rows_sum = rows_sum + grad[h2, 0:64, :] + grad[h2, 64:128, :]
    point = point[:C] + point[C:]
    point = point + swap(point)
    bias_term = jnp.sum(rows_sum, axis=1, keepdims=True)
    sums_of = [red1, red2, red3, red4]
    folded = jnp.concatenate([point[: C // 2, :C], point[C // 2:, :C]], 1)
    bias_row = jnp.broadcast_to(bias_term, (C, 128)).T[:8]
    first = jnp.concatenate([folded, jnp.concatenate([bias_row, bias_row], 1)], 0)
    reduces = []

    def send_sum(number, rows):
        own, ids = sum_steps[number]
        ref = sums_of[number]
        ref[pl.ds(own, 1)] = rows[None]
        copies = [
            pltpu.make_async_remote_copy(
                src_ref=ref.at[own],
                dst_ref=ref.at[own],
                send_sem=rsend_sem.at[number, n],
                recv_sem=rrecv_sem.at[number, n],
                device_id=device,
                device_id_type=MESH,
            )
            for n, device in enumerate(ids)
        ]
        for copy in copies:
            copy.start()
        reduces.append(copies)

    def take_sum(number):
        for copy in reduces[number]:
            copy.wait_recv()
        ref = sums_of[number]
        rows = ref[0]
        for n in range(1, len(reduces[number]) + 1):
            rows = rows + ref[n]
        return rows

    send_sum(0, first)

    for h4 in range(PAIRS // 2):
        mapped = point_map(wbwd[...], ghl[h4 * 256:h4 * 256 + 256, :])
        for k in range(2):
            h2 = 2 * h4 + k
            base[h2] = mapped[128 * k:128 * k + 128] + grad[h2]
    send_sum(1, take_sum(0))
    send_sum(2, take_sum(1))

    gtotal = send3[0]
    for n, (dl, ds) in enumerate(steps):
        copies3[n].wait_recv()
        gtotal = gtotal + recv3[dl * 2 + ds]

    def unpacked(rows, b):
        part = rows[8 * b:8 * b + 8]
        return jnp.concatenate([part[:, :C], part[:, C:]], 0)

    gmodes = [unpacked(gtotal, b) for b in range(4)]
    backs = []
    for b in range(4):
        rows = gtotal[8 * b:8 * b + 8]
        turned = swap(rows)
        both = []
        for ii in range(2):
            lhs = stacked(jnp.where(left8, rows, turned) if ii == 0 else jnp.where(left8, turned, rows))
            maps = wmix[b * 16 + ii * 8:b * 16 + ii * 8 + 8].reshape(8 * C, 2 * C)
            out = dot_nt(lhs, maps)
            out = out[:8] + out[8:]
            kept = jnp.zeros((8, 2 * C), F32)
            for j2 in range(4):
                part = out[:, 128 * j2:128 * j2 + 128]
                kept = jnp.where(row8 - half8 == 2 * j2, part, kept)
            both.append(kept + swap(kept))
        backs.append(jnp.where(left8, both[0], both[1]))
    send4[...] = jnp.concatenate(backs, 0) - gtotal
    copies4 = exchange(3, lambda n: send4, recv4, ahead)
    for copy in copies4:
        copy.start()

    send_sum(3, take_sum(2))

    def outer(g, turned):
        for k in range(8):
            for b in range(4):
                rows = turned[8 * b:8 * b + 8]
                column = jnp.concatenate([rows[:, k:k + 1], rows[:, C + k:C + k + 1]], 0)
                out_gw[b, g * 8 + k] = column * gmodes[b]
        return pltpu.roll(turned, 2 * C - 8, axis=1)

    lax.fori_loop(0, C // 8, outer, coarse[...])
    for copy in copies4:
        copy.wait_recv()
    rows = take_sum(3)
    out_gp[...] = jnp.concatenate([rows[: C // 2, :C], rows[: C // 2, C:]], 0)
    out_gb[...] = rows[C // 2:C // 2 + 1, :C]
    for copy in copies1 + copies2 + copies3 + copies4 + sum(reduces, []):
        copy.wait_send()


def last_kernel(
    base, recv4, send4, gw, gp, gb, lat_tab, join_tab, out_field, out_ga, out_gd, out_gp, out_gb, dup, obuf, sem
):
    stores = []

    def store(src, dst):
        stores.append(pltpu.make_async_copy(src, dst, sem.at[len(stores)]))
        stores[-1].start()

    store(gw.at[0], out_ga)
    for b in range(3):
        store(gw.at[1 + b], out_gd.at[b])
    store(gp, out_gp)
    store(gb, out_gb)
    left = lax.broadcasted_iota(jnp.int32, (32, 2 * C), 1) < C
    lat_join(recv4, send4, dup, left)
    for h2 in range(PAIRS):
        cells = base[h2] + lon_join(h2, dup, lat_tab, join_tab)
        chunk, row = h2 // 4, (h2 % 4) * 2
        flat = obuf.at[chunk].reshape(C * 8, W)
        for p in range(2):
            flat[pl.ds(row + p, C, stride=8), :] = cells[64 * p:64 * p + 64]
        if h2 % 4 == 3:
            store(obuf.at[chunk], out_field.at[:, pl.ds(8 * chunk, 8), :])
    for copy in stores:
        copy.wait()


def body(field, cotangent, w_approx, w_detail, w_point, bias):
    lat_tab, split_tab, join_tab = tables()
    wa = jnp.transpose(w_approx, (0, 2, 3, 1)).reshape(C, 16, C)
    wd = jnp.transpose(w_detail, (0, 1, 3, 4, 2)).reshape(3, C, 16, C)
    anywhere = pl.BlockSpec(memory_space=pl.ANY)
    vmem = pltpu.VMEM
    block = (32, 128)
    hbm = pl.BlockSpec(memory_space=pltpu.HBM)
    results = pl.pallas_call(
        kernel,
        out_shape=(
            vmem((PAIRS, 2 * C, W), F32),
            vmem((8,) + block, F32),
            vmem(block, F32),
            vmem((4, C, 16, C), F32),
            vmem((C, C), F32),
            vmem((1, C), F32),
            vmem((PAIRS * 16, 2 * C), F32),
            vmem((96, W), F32),
        ),
        in_specs=[hbm] * 9,
        out_specs=(pl.BlockSpec(memory_space=vmem),) * 8,
        scratch_shapes=[
            vmem((4, C, 8, W), F32),
            vmem((4, C, 8, W), F32),
            vmem((4, C, 16, C), F32),
            vmem((C, C), F32),
            vmem((1, C), F32),
            vmem((64, 2 * W), F32),
            vmem((C, C, 2 * C), BF16),
            vmem((3 * C, C), BF16),
            vmem((3 * C, C), BF16),
            vmem((PAIRS, 2 * C, W), F32),
            vmem((PAIRS * 2 * C, 2 * W), BF16),
            vmem((PAIRS * 2 * C, 2 * W), BF16),
            vmem((PAIRS, 32, 2 * C), F32),
            vmem((16, 32, 2 * C), F32),
            vmem((8,) + block, F32),
            vmem(block, F32),
            vmem((8,) + block, F32),
            vmem((8,) + block, F32),
            vmem((8,) + block, F32),
            vmem((8,) + block, F32),
            vmem(block, F32),
            vmem((8, 40, 128), F32),
            vmem((4, 40, 128), F32),
            vmem((4, 40, 128), F32),
            vmem((4, 40, 128), F32),
            pltpu.SemaphoreType.DMA((7,)),
            pltpu.SemaphoreType.DMA((8,)),
            pltpu.SemaphoreType.DMA((4, 7)),
            pltpu.SemaphoreType.DMA((4, 7)),
            pltpu.SemaphoreType.DMA((4, 7)),
            pltpu.SemaphoreType.DMA((4, 7)),
        ],
        compiler_params=pltpu.CompilerParams(
            collective_id=0, has_side_effects=True, vmem_limit_bytes=48 * 1024 * 1024
        ),
    )(
        *[
            pltpu.with_memory_space_constraint(x, pltpu.HBM)
            for x in (
                field,
                cotangent,
                wa,
                wd,
                w_point,
                bias.reshape(1, C),
                jnp.asarray(lat_tab),
                jnp.asarray(split_tab),
                jnp.asarray(join_tab),
            )
        ]
    )
    gfield, ga, gd, gp, gb = pl.pallas_call(
        last_kernel,
        out_shape=(
            jax.ShapeDtypeStruct((C, H, W), F32),
            jax.ShapeDtypeStruct((C, 16, C), F32),
            jax.ShapeDtypeStruct((3, C, 16, C), F32),
            jax.ShapeDtypeStruct((C, C), F32),
            jax.ShapeDtypeStruct((1, C), F32),
        ),
        in_specs=[pl.BlockSpec(memory_space=vmem)] * 8,
        out_specs=(anywhere,) * 5,
        scratch_shapes=[
            vmem((16, 32, 2 * C), F32),
            vmem((4, C, 8, W), F32),
            pltpu.SemaphoreType.DMA((10,)),
        ],
        compiler_params=pltpu.CompilerParams(vmem_limit_bytes=32 * 1024 * 1024),
    )(*[pltpu.with_memory_space_constraint(x, vmem) for x in results])
    ga = jnp.transpose(ga.reshape(C, 2, 8, C), (0, 3, 1, 2))
    gd = jnp.transpose(gd.reshape(3, C, 2, 8, C), (0, 1, 4, 2, 3))
    return gfield, ga, gd, gp, gb.reshape(C)


def solution(mesh):
    placed = (
        P(None, "lat", "lon"),
        P(None, "lat", "lon"),
        P(None, None, "lat", "lon"),
        P(None, None, None, "lat", "lon"),
        P(),
        P(),
    )
    return jax.shard_map(
        body,
        mesh=mesh,
        in_specs=placed,
        out_specs=(
            P(None, "lat", "lon"),
            P(None, None, "lat", "lon"),
            P(None, None, None, "lat", "lon"),
            P(),
            P(),
        ),
        check_vma=False,
    )
```
